128 devices in a mesh: prow: 8 (over z, core), pcol: 16 (over x, y).
Axes of the slice: x: 4, y: 4, z: 4, core: 2. Of those that a mesh axis runs over, the one named last changes fastest.
Arguments:
- rhs: float32 [4, 8, 16, 128, 256], P(None, 'prow', 'pcol'), may hold values from -6 to 6
- dinv: float32 [4, 8, 16, 128, 128], P(None, 'prow', 'pcol'), as said below
- blocks: float32 [8, 16, 6, 32, 128, 128], P('prow', 'pcol'), may hold values from -0.046875 to 0.046875
- targets: int32 [8, 16, 6, 32], P('prow', 'pcol'), may hold values from -1 to 7, as said below
- sources: int32 [8, 16, 6, 32], P('prow', 'pcol'), may hold values from 0 to 15
Outputs:
- forward: float32 [4, 8, 16, 128, 256], P(None, 'prow', 'pcol')
- solution: float32 [4, 8, 16, 128, 256], P(None, 'prow', 'pcol')
The draws below stay inside these ranges and needn't reach their ends.
Inputs may be any that keep to these rules, and one draw needn't show every extreme that they name: `dinv`: each diagonal-block inverse is lower triangular with diagonal entries between 0.5 and 1.5. `targets`: in each device's 32 slots of a level pair the live slots (not -1) come first; for every level pair some device has all 32 slots live.
All inputs are finite; a program needn't handle non-finite values.
Results may differ from the reference program's by a relative error of at most 0.0003.
Values sent between devices are 32-bit elements; how exact they have to be, the bound alone decides.
No kernel may reach another device: no remote copies, remote signals or barrier semaphores. Data moves between devices by JAX's collectives and lax.ppermute only.
A program may use at most 128 MiB of HBM per device.

```python
import math
import jax
import jax.numpy as jnp
from jax import lax

W = 128
R = 256
LEV = 4
NB = 32
PAIRS = 6
GRID_ROWS = 8
GRID_COLS = 16


def draw_dinv(key, part):
    key = jax.random.fold_in(key, 7)
    first, second = jax.random.split(key)
    shape = (LEV, GRID_ROWS, GRID_COLS, W, W)
    lower = (jnp.arange(W)[:, None] > jnp.arange(W)[None, :]).astype(jnp.float32)
    identity = jnp.eye(W, dtype=jnp.float32)
    spread = jax.random.normal(first, shape, jnp.float32) * (0.5 / math.sqrt(W))
    diagonal = jax.random.uniform(second, shape[:-1], jnp.float32, 0.5, 1.5)
    return spread * lower + identity * diagonal[..., None]


def draw_targets(key, part):
    key = jax.random.fold_in(key, 11)
    first, second, third = jax.random.split(key, 3)
    devices = GRID_ROWS * GRID_COLS
    counts = jax.random.randint(first, (GRID_ROWS, GRID_COLS, PAIRS), max(NB // 4, 1), NB + 1)
    fullest = jax.random.randint(second, (PAIRS,), 0, devices)
    flat = jnp.arange(devices, dtype=jnp.int32).reshape(GRID_ROWS, GRID_COLS)
    counts = jnp.where(flat[:, :, None] == fullest[None, None, :], NB, counts)
    slots = jnp.arange(NB, dtype=jnp.int32)
    picks = jax.random.randint(third, (GRID_ROWS, GRID_COLS, PAIRS, NB), 0, GRID_ROWS)
    return jnp.where(slots < counts[..., None], picks, -1).astype(jnp.int32)


def place_ends(drawn, rng, least, largest):
    longest = drawn.shape.index(max(drawn.shape))
    spots = []
    for shift in (0, 1):
        where = [jax.random.randint(jax.random.fold_in(rng, axis), (), 0, length) for axis, length in enumerate(drawn.shape)]
        where[longest] = (where[longest] + shift) % drawn.shape[longest]
        spots.append(tuple(where))
    return drawn.at[spots[0]].set(least).at[spots[1]].set(largest)


def shard_levels(stream_key, dims, cuts, smallest, largest):
    level, own = 1.0, jax.random.fold_in(stream_key, 6)
    for dim, blocks in cuts:
        heights = jnp.exp(jax.random.uniform(jax.random.fold_in(own, dim), (blocks,), jnp.float32, smallest / len(cuts), largest / len(cuts)))
        level = level * jnp.repeat(heights, dims[dim] // blocks).reshape([-1 if axis == dim else 1 for axis in range(len(dims))])
    return level


def noise(rng, extent, width, reach, cuts=(), kind=jnp.bfloat16):
    values = width * jax.random.normal(rng, extent, jnp.float32)
    if cuts:
        values = values * shard_levels(rng, extent, cuts, -0.22, 0.18)
    return jnp.clip(values, -reach, reach).astype(kind)


def setup_inputs(seed: int = 0) -> dict:
    arg_keys = jax.random.split(jax.random.key(seed), 6)
    return {
        "rhs": noise(arg_keys[0], (LEV, GRID_ROWS, GRID_COLS, W, R), 1.0, 6.0, ((1, 8), (2, 16)), jnp.float32),
        "dinv": draw_dinv(jax.random.fold_in(arg_keys[5], 71), 0),
        "blocks": noise(arg_keys[2], (GRID_ROWS, GRID_COLS, PAIRS, NB, W, W), (W * NB * LEV) ** -0.5, 0.046875, ((0, 8), (1, 16)), jnp.float32),
        "targets": draw_targets(jax.random.fold_in(arg_keys[5], 71), 0),
        "sources": place_ends(jax.random.randint(arg_keys[4], (GRID_ROWS, GRID_COLS, PAIRS, NB), 0, GRID_COLS), jax.random.fold_in(arg_keys[4], 1), 0, GRID_COLS - 1).astype(jnp.int32),
    }


def pair_index(high, low):
    return high * (high - 1) // 2 + low


def reference(rhs, dinv, blocks, targets, sources):
    best = lax.Precision.HIGHEST
    row_ids = jnp.arange(GRID_ROWS, dtype=jnp.int32)
    col_ids = jnp.arange(GRID_COLS, dtype=jnp.int32)
    solved = []
    for level in range(LEV):
        total = jnp.zeros((GRID_ROWS, GRID_COLS, W, R), jnp.float32)
        for lower in range(level):
            index = pair_index(level, lower)
            earlier = solved[lower]

            def add_row(carry, owner):
                chosen = earlier[owner][sources[owner, :, index, :]]
                product = jnp.einsum("cbij,cbjk->cbik", blocks[owner, :, index], chosen, precision=best)
                hits = (targets[owner, :, index, :][None, :, :] == row_ids[:, None, None]).astype(jnp.float32)
                return carry + jnp.einsum("tcb,cbik->tcik", hits, product, precision=best), None

            total, _ = lax.scan(add_row, total, row_ids)
        solved.append(jnp.einsum("rcij,rcjk->rcik", dinv[level], rhs[level] - total, precision=best))
    forward = jnp.stack(solved)
    result = [None] * LEV
    for level in reversed(range(LEV)):
        total = jnp.zeros((GRID_ROWS, GRID_COLS, W, R), jnp.float32)
        for higher in range(level + 1, LEV):
            index = pair_index(higher, level)
            later = result[higher]

            def row_terms(owner):
                aims = targets[owner, :, index, :]
                chosen = later[jnp.maximum(aims, 0), col_ids[:, None]]
                product = jnp.einsum("cbji,cbjk->cbik", blocks[owner, :, index], chosen, precision=best)
                live = (aims >= 0).astype(jnp.float32)
                hits = (sources[owner, :, index, :][None, :, :] == col_ids[:, None, None]).astype(jnp.float32) * live[None]
                return jnp.einsum("scb,cbik->sik", hits, product, precision=best)

            total = total + lax.map(row_terms, row_ids)
        result[level] = jnp.einsum("rcji,rcjk->rcik", dinv[level], forward[level] - total, precision=best)
    return forward, jnp.stack(result)
```

```python
import functools

import jax
import jax.numpy as jnp
from jax import lax
from jax.experimental import pallas as pl
from jax.experimental.pallas import tpu as pltpu
from jax.sharding import PartitionSpec as P

W = 128
R = 256
LEV = 4
NZ, NC, NX, NY = 4, 2, 4, 4
CHUNK = 8
BOTH = ("prow", "pcol")


def pair_index(high, low):
    return high * (high - 1) // 2 + low


def device(z, c, x, y):
    return (z % NZ * NC + c) * NX * NY + x % NX * NY + y % NY


def shift_plane(value, step, phase):
    pairs = []
    for z in range(NZ):
        for c in range(NC):
            for x in range(NX):
                for y in range(NY):
                    if c == phase:
                        there = device(z, c, x + step, y)
                    else:
                        there = device(z, c, x, y + step)
                    pairs.append((device(z, c, x, y), there))
    return lax.ppermute(value, BOTH, pairs)


def shift_z(value, step):
    pairs = [(z * NC + c, (z + step) % NZ * NC + c) for z in range(NZ) for c in range(NC)]
    return lax.ppermute(value, "prow", pairs)


def swap_core(value):
    pairs = [(z * NC + c, z * NC + 1 - c) for z in range(NZ) for c in range(NC)]
    return lax.ppermute(value, "prow", pairs)


def split(value):
    high = value.astype(jnp.bfloat16)
    low = (value - high.astype(jnp.float32)).astype(jnp.bfloat16)
    return high, low


def pair_kernel(n_in, n_out, flip, has_init, slots, gathered, *refs):
    take, put, live = slots
    count = gathered
    vectors = refs[:count]
    blocks = refs[count]
    refs = refs[count + 1 :]
    init = refs[:n_out] if has_init else ()
    refs = refs[n_out:] if has_init else refs
    outs, (halves, total) = refs[:n_out], refs[n_out:]
    step = pl.program_id(0)

    @pl.when(step == 0)
    def _():
        per = n_in // count
        for k in range(n_in):
            high, low = split(vectors[k // per][k % per])
            halves[k, :W] = high
            halves[k, W:] = low
        per = total.shape[0] // n_out
        for k in range(n_out):
            if has_init:
                total[k * per : (k + 1) * per] = init[k][...]
            else:
                total[k * per : (k + 1) * per] = jnp.zeros((per, W, R), jnp.float32)

    for j in range(CHUNK):
        slot = step * CHUNK + j
        block = blocks[0, j]
        block = jnp.where(live[slot] > 0, block, 0.0)
        if flip:
            block = block.T
        high, low = split(block)
        left = jnp.concatenate(
            [jnp.concatenate([high, high], axis=1), jnp.concatenate([low, low], axis=1)], axis=0
        )
        product = jnp.dot(left, halves[take[slot]], preferred_element_type=jnp.float32)
        total[put[slot]] += product[:W] + product[W:]

    @pl.when(step == pl.num_programs(0) - 1)
    def _():
        per = total.shape[0] // n_out
        for k in range(n_out):
            outs[k][...] = total[k * per : (k + 1) * per]


def pair_product(index, flip, take, put, live, vectors, panels, init, n_out, total):
    n_in = sum(v.shape[0] for v in vectors)
    nb = panels.shape[1]
    per = total // n_out

    def kernel(take_ref, put_ref, live_ref, *refs):
        pair_kernel(n_in, n_out, flip, init is not None, (take_ref, put_ref, live_ref), len(vectors), *refs)

    def whole(step, *_):
        return (0, 0, 0)

    inits = [] if init is None else list(init)
    return pl.pallas_call(
        kernel,
        grid_spec=pltpu.PrefetchScalarGridSpec(
            num_scalar_prefetch=3,
            grid=(nb // CHUNK,),
            in_specs=[pl.BlockSpec(v.shape, whole) for v in vectors]
            + [pl.BlockSpec((1, CHUNK, W, W), lambda step, *_: (index, step, 0, 0))]
            + [pl.BlockSpec(v.shape, whole) for v in inits],
            out_specs=[pl.BlockSpec((per, W, R), whole)] * n_out,
            scratch_shapes=[
                pltpu.VMEM((n_in, 2 * W, R), jnp.bfloat16),
                pltpu.VMEM((total, W, R), jnp.float32),
            ],
        ),
        out_shape=[jax.ShapeDtypeStruct((per, W, R), jnp.float32)] * n_out,
        compiler_params=pltpu.CompilerParams(vmem_limit_bytes=40 * 1024 * 1024),
        cost_estimate=pl.CostEstimate(
            flops=nb * 8 * W * W * R, bytes_accessed=nb * W * W * 4, transcendentals=0
        ),
    )(take, put, live, *vectors, panels, *inits)


def solve_kernel(flip, terms, inverse, base, *refs):
    out = refs[-1]
    value = base[...]
    if terms:
        gone = refs[0][...]
        for ref in refs[1:terms]:
            gone = gone + ref[...]
        value = value - gone
    matrix = inverse[...]
    if flip:
        matrix = matrix.T
    out[...] = jnp.dot(
        matrix, value, precision=lax.Precision.HIGHEST, preferred_element_type=jnp.float32
    )


def solve(flip, inverse, base, gone):
    return pl.pallas_call(
        functools.partial(solve_kernel, flip, len(gone)),
        out_shape=jax.ShapeDtypeStruct((W, R), jnp.float32),
        cost_estimate=pl.CostEstimate(flops=12 * W * W * R, bytes_accessed=4 * W * R, transcendentals=0),
    )(inverse, base, *gone)


def gather_plane(value):
    units = jnp.stack([value] + [shift_plane(value, d, 0) for d in (1, 2, 3)])
    return [units] + [shift_plane(units, d, 1) for d in (1, 2, 3)]


def scatter_plane(groups):
    units = groups[0]
    for d in (1, 2, 3):
        units = units + shift_plane(groups[d], d, 0)
    return [units[0]] + [shift_plane(units[d], d, 1) for d in (1, 2, 3)]


def scatter_z(mine, other):
    units = mine + swap_core(other)
    return [units[0]] + [shift_z(units[d], d) for d in (1, 2, 3)]


def gather_z(value):
    units = jnp.stack([value] + [shift_z(value, d) for d in (1, 2, 3)])
    return [units, swap_core(units)]


def body(rhs, dinv, blocks, targets, sources):
    right = rhs[:, 0, 0]
    inverse = dinv[:, 0, 0]
    panels = blocks[0, 0]
    aims = targets[0, 0]
    anchor = sources[0, 0]
    row = lax.axis_index("prow")
    col = lax.axis_index("pcol")
    z, core = row // NC, row % NC
    x, y = col // NY, col % NY
    live = (aims >= 0).astype(jnp.int32)
    rows = jnp.maximum(aims, 0)
    off_x = (x - anchor // NY) % NX
    off_y = (y - anchor % NY) % NY
    near_x, near_y = (-off_x) % NX, (-off_y) % NY
    first = core == 0
    take_plane = jnp.where(first, off_y * NX + off_x, off_x * NY + off_y)
    put_plane = jnp.where(first, near_x * NY + near_y, near_y * NX + near_x)
    off_z = (z - rows // NC) % NZ
    across = (rows % NC != core).astype(jnp.int32) * NZ
    take_z = across + off_z
    put_z = across + (-off_z) % NZ

    def forth(high, low, vectors, init):
        index = pair_index(high, low)
        return pair_product(
            index, False, take_plane[index], put_z[index], live[index], vectors, panels, init, 2, 8
        )

    def back(high, low, vectors, init):
        index = pair_index(high, low)
        return pair_product(
            index, True, take_z[index], put_plane[index], live[index], vectors, panels, init, 4, 16
        )

    solved = [None] * LEV
    sums = [None] * LEV
    for level in range(LEV):
        gone = [] if level == 0 else scatter_z(*sums[level])
        solved[level] = solve(False, inverse[level], right[level], gone)
        if level + 1 < LEV:
            vectors = gather_plane(solved[level])
            for high in range(level + 1, LEV):
                sums[high] = forth(high, level, vectors, sums[high])
    result = [None] * LEV
    sums = [None] * LEV
    for level in reversed(range(LEV)):
        gone = [] if level == LEV - 1 else scatter_plane(sums[level])
        result[level] = solve(True, inverse[level], solved[level], gone)
        if level > 0:
            vectors = gather_z(result[level])
            for low in reversed(range(level)):
                sums[low] = back(level, low, vectors, sums[low])
    forward = jnp.stack(solved)[:, None, None]
    solution = jnp.stack(result)[:, None, None]
    return (forward, solution)


def solution(mesh):
    placed = (
        P(None, "prow", "pcol", None, None),
        P(None, "prow", "pcol", None, None),
        P("prow", "pcol", None, None, None, None),
        P("prow", "pcol", None, None),
        P("prow", "pcol", None, None),
    )
    return jax.shard_map(
        body,
        mesh=mesh,
        in_specs=placed,
        out_specs=(P(None, "prow", "pcol", None, None), P(None, "prow", "pcol", None, None)),
        check_vma=False,
    )
```

```python
import functools

import jax
import jax.numpy as jnp
from jax import lax
from jax.experimental import pallas as pl
from jax.experimental.pallas import tpu as pltpu
from jax.sharding import PartitionSpec as P

W = 128
R = 256
LEV = 4
NZ, NC, NX, NY = 4, 2, 4, 4
BOTH = ("prow", "pcol")
PLAIN = (1, 2, 3)
FAR_FIRST = (2, 1, 3)


def pair_index(high, low):
    return high * (high - 1) // 2 + low


def device(z, c, x, y):
    return (z % NZ * NC + c) * NX * NY + x % NX * NY + y % NY


def shift_plane(value, step, phase):
    pairs = []
    for z in range(NZ):
        for c in range(NC):
            for x in range(NX):
                for y in range(NY):
                    if c == phase:
                        there = device(z, c, x + step, y)
                    else:
                        there = device(z, c, x, y + step)
                    pairs.append((device(z, c, x, y), there))
    return lax.ppermute(value, BOTH, pairs)


def shift_z(value, step):
    pairs = [(z * NC + c, (z + step) % NZ * NC + c) for z in range(NZ) for c in range(NC)]
    return lax.ppermute(value, "prow", pairs)


def swap_core(value):
    pairs = [(z * NC + c, z * NC + 1 - c) for z in range(NZ) for c in range(NC)]
    return lax.ppermute(value, "prow", pairs)


def split(value):
    high = value.astype(jnp.bfloat16)
    low = (value - high.astype(jnp.float32)).astype(jnp.bfloat16)
    return high, low


def near(value):
    return pltpu.with_memory_space_constraint(value, pltpu.VMEM)


def far(value):
    return pltpu.with_memory_space_constraint(value, pltpu.HBM)


def fast_call(kernel, shapes, operands, scalars, scratch, flops):
    return pl.pallas_call(
        kernel,
        in_specs=[pl.BlockSpec(memory_space=pltpu.SMEM)] * len(scalars)
        + [pl.BlockSpec(memory_space=pltpu.VMEM)] * len(operands),
        out_specs=[pl.BlockSpec(memory_space=pltpu.VMEM)] * len(shapes),
        out_shape=[pltpu.VMEM(shape, jnp.float32) for shape in shapes],
        scratch_shapes=scratch,
        compiler_params=pltpu.CompilerParams(vmem_limit_bytes=16 * 1024 * 1024),
        cost_estimate=pl.CostEstimate(flops=flops, bytes_accessed=4096, transcendentals=0),
    )(*scalars, *[near(value) for value in operands])


def pair_kernel(index, n_in, n_out, flip, has_init, waits, take, put, live, *refs):
    vectors, refs = refs[:n_in], refs[n_in:]
    blocks, refs = refs[0], refs[1:]
    init, refs = (refs[:n_out], refs[n_out:]) if has_init else ((), refs)
    refs = refs[waits:]
    outs, halves, total = refs[:n_out], refs[n_out], refs[n_out + 1]
    per = vectors[0].shape[0]
    for k in range(n_in * per):
        high, low = split(vectors[k // per][k % per])
        halves[k, :W] = high
        halves[k, W:] = low
    per = outs[0].shape[0]
    for k in range(n_out):
        if has_init:
            total[k * per : (k + 1) * per] = init[k][...]
        else:
            total[k * per : (k + 1) * per] = jnp.zeros((per, W, R), jnp.float32)
    for slot in range(blocks.shape[1]):
        block = jnp.where(live[slot] > 0, blocks[index, slot], 0.0)
        if flip:
            block = block.T
        high, low = split(block)
        left = jnp.concatenate(
            [jnp.concatenate([high, high], axis=1), jnp.concatenate([low, low], axis=1)], axis=0
        )
        product = jnp.dot(left, halves[take[slot]], preferred_element_type=jnp.float32)
        total[put[slot]] += product[:W] + product[W:]
    for k in range(n_out):
        outs[k][...] = total[k * per : (k + 1) * per]


def pair_product(index, flip, scalars, vectors, blocks, init, after, n_out, total):
    n_in = len(vectors)
    units = n_in * vectors[0].shape[0]
    return fast_call(
        functools.partial(pair_kernel, index, n_in, n_out, flip, init is not None, len(after)),
        [(total // n_out, W, R)] * n_out,
        [*vectors, blocks, *(init or ()), *after],
        scalars,
        [pltpu.VMEM((units, 2 * W, R), jnp.bfloat16), pltpu.VMEM((total, W, R), jnp.float32)],
        blocks.shape[1] * 8 * W * W * R,
    )


def dot(left, right):
    return jnp.dot(
        left, right, precision=lax.Precision.HIGHEST, preferred_element_type=jnp.float32
    )


def solve_kernel(level, flip, stacked, terms, inverse, base, *refs):
    value = base[level] if stacked else base[...]
    if terms:
        gone = refs[0][...]
        for ref in refs[1:terms]:
            gone = gone + ref[...]
        value = value - gone
    outs = refs[terms:]
    for flipped, out in zip(flip, outs):
        matrix = inverse[level]
        value = dot(matrix.T if flipped else matrix, value)
        out[...] = value


def solve(level, flip, inverse, base, gone):
    return fast_call(
        functools.partial(solve_kernel, level, flip, base.ndim == 3, len(gone)),
        [(W, R)] * len(flip),
        [inverse, base, *gone],
        [],
        [],
        12 * W * W * R,
    )


def add_kernel(terms, waits, *refs):
    for k, out in enumerate(refs[terms + waits :]):
        value = refs[0][k]
        for ref in refs[1:terms]:
            value = value + ref[k]
        out[...] = value


def add_units(parts, after):
    return fast_call(
        functools.partial(add_kernel, len(parts), len(after)),
        [(W, R)] * 4,
        [*parts, *after],
        [],
        [],
        len(parts) * 4 * W * R,
    )


def first_kernel(inverse, base, out, matrix, value, sems):
    copies = [
        pltpu.make_async_copy(inverse.at[0], matrix, sems.at[0]),
        pltpu.make_async_copy(base.at[0], value, sems.at[1]),
    ]
    for copy in copies:
        copy.start()
    for copy in copies:
        copy.wait()
    out[...] = dot(matrix[...], value[...])


def first_solve(inverse, base):
    return pl.pallas_call(
        first_kernel,
        in_specs=[pl.BlockSpec(memory_space=pl.ANY)] * 2,
        out_specs=pl.BlockSpec(memory_space=pltpu.VMEM),
        out_shape=pltpu.VMEM((W, R), jnp.float32),
        scratch_shapes=[
            pltpu.VMEM((W, W), jnp.float32),
            pltpu.VMEM((W, R), jnp.float32),
            pltpu.SemaphoreType.DMA((2,)),
        ],
        compiler_params=pltpu.CompilerParams(vmem_limit_bytes=16 * 1024 * 1024),
    )(far(inverse), far(base))


def load_kernel(blocks, after, out, sems):
    copies = [
        pltpu.make_async_copy(blocks.at[k], out.at[k], sems.at[k]) for k in range(blocks.shape[0])
    ]
    for copy in copies:
        copy.start()
    for copy in copies:
        copy.wait()


def load(blocks, after):
    return pl.pallas_call(
        load_kernel,
        in_specs=[pl.BlockSpec(memory_space=pl.ANY), pl.BlockSpec(memory_space=pltpu.VMEM)],
        out_specs=pl.BlockSpec(memory_space=pltpu.VMEM),
        out_shape=pltpu.VMEM(blocks.shape, jnp.float32),
        scratch_shapes=[pltpu.SemaphoreType.DMA((blocks.shape[0],))],
        compiler_params=pltpu.CompilerParams(vmem_limit_bytes=16 * 1024 * 1024),
        cost_estimate=pl.CostEstimate(
            flops=0, bytes_accessed=blocks.size * 4, transcendentals=0
        ),
    )(far(blocks), near(after))


def gather_plane(value):
    units = jnp.stack([value] + [shift_plane(value, d, 0) for d in PLAIN])
    return [units] + [shift_plane(units, d, 1) for d in PLAIN]


def scatter_plane(groups, beside):
    first = [shift_plane(groups[k], d, 0) for k, d in enumerate(FAR_FIRST, 1)]
    units = add_units([groups[0]] + first, beside(first[0]))
    return [units[0]] + [shift_plane(units[d], d, 1) for d in PLAIN]


def scatter_z(mine, other):
    units = add_units([mine, swap_core(other)], [])
    return [units[0]] + [shift_z(units[d], d) for d in PLAIN]


def gather_z(value):
    units = jnp.stack([value] + [shift_z(value, d) for d in PLAIN])
    return [units, swap_core(units)]


def place(offset, order):
    spot = jnp.zeros_like(offset)
    for k, d in enumerate(order, 1):
        spot = jnp.where(offset == d, k, spot)
    return spot


def body(rhs, dinv, blocks, targets, sources):
    right = rhs[:, 0, 0]
    inverse = dinv[:, 0, 0]
    aims = targets[0, 0]
    anchor = sources[0, 0]
    row = lax.axis_index("prow")
    col = lax.axis_index("pcol")
    z, core = row // NC, row % NC
    x, y = col // NY, col % NY
    live = (aims >= 0).astype(jnp.int32)
    rows = jnp.maximum(aims, 0)
    off_x = (x - anchor // NY) % NX
    off_y = (y - anchor % NY) % NY
    off_z = (z - rows // NC) % NZ
    first = core == 0
    to_x, to_y, to_z = (-off_x) % NX, (-off_y) % NY, (-off_z) % NZ
    take_plane = jnp.where(first, off_y * NX + off_x, off_x * NY + off_y)
    put_plane = jnp.where(
        first, place(to_x, FAR_FIRST) * NY + to_y, place(to_y, FAR_FIRST) * NX + to_x
    )
    across = (rows % NC != core).astype(jnp.int32) * NZ
    take_z = across + off_z
    put_z = across + to_z

    def forth(high, low, vectors, init):
        index = pair_index(high, low)
        scalars = (take_plane[index], put_z[index], live[index])
        return pair_product(index, False, scalars, vectors, panels, init, (), 2, 8)

    def back(high, low, vectors, init, after):
        index = pair_index(high, low)
        scalars = (take_z[index], put_plane[index], live[index])
        return pair_product(index, True, scalars, vectors, panels, init, after, 4, 16)

    top = LEV - 1
    solved = [None] * LEV
    result = [None] * LEV
    sums = [None] * LEV
    for level in range(LEV):
        gone = [] if level == 0 else scatter_z(*sums[level])
        if level == top:
            solved[level], result[level] = solve(level, (False, True), inverse, right, gone)
            break
        if level == 0:
            solved[level] = first_solve(inverse, right)
        else:
            (solved[level],) = solve(level, (False,), inverse, right, gone)
        vectors = gather_plane(solved[level])
        if level == 0:
            panels = load(blocks[0, 0], vectors[0])
        for high in range(level + 1, LEV):
            sums[high] = forth(high, level, vectors, sums[high])
    sums = [None] * LEV
    for level in reversed(range(1, LEV)):
        vectors = gather_z(result[level])

        def beside(held):
            done = []
            for low in reversed(range(level - 1)):
                sums[low] = back(level, low, vectors, sums[low], (held,))
                done += sums[low][:1]
            return done

        gone = scatter_plane(back(level, level - 1, vectors, sums[level - 1], ()), beside)
        (result[level - 1],) = solve(level - 1, (True,), inverse, solved[level - 1], gone)
    forward = jnp.stack(solved)[:, None, None]
    solution = jnp.stack(result)[:, None, None]
    return (forward, solution)


def solution(mesh):
    placed = (
        P(None, "prow", "pcol", None, None),
        P(None, "prow", "pcol", None, None),
        P("prow", "pcol", None, None, None, None),
        P("prow", "pcol", None, None),
        P("prow", "pcol", None, None),
    )
    return jax.shard_map(
        body,
        mesh=mesh,
        in_specs=placed,
        out_specs=(P(None, "prow", "pcol", None, None), P(None, "prow", "pcol", None, None)),
        check_vma=False,
    )
```

```python
import functools

import jax
import jax.numpy as jnp
from jax import lax
from jax.experimental import pallas as pl
from jax.experimental.pallas import tpu as pltpu
from jax.sharding import PartitionSpec as P

W = 128
R = 256
LEV = 4
NZ, NC, NX, NY = 4, 2, 4, 4
BOTH = ("prow", "pcol")
UNROLL = 16
PLAIN = (1, 2, 3)
FAR_FIRST = (2, 1, 3)


def pair_index(high, low):
    return high * (high - 1) // 2 + low


def device(z, c, x, y):
    return (z % NZ * NC + c) * NX * NY + x % NX * NY + y % NY


def shift_plane(value, step, phase):
    pairs = []
    for z in range(NZ):
        for c in range(NC):
            for x in range(NX):
                for y in range(NY):
                    if c == phase:
                        there = device(z, c, x + step, y)
                    else:
                        there = device(z, c, x, y + step)
                    pairs.append((device(z, c, x, y), there))
    return lax.ppermute(value, BOTH, pairs)


def shift_z(value, step):
    pairs = [(z * NC + c, (z + step) % NZ * NC + c) for z in range(NZ) for c in range(NC)]
    return lax.ppermute(value, "prow", pairs)


def swap_core(value):
    pairs = [(z * NC + c, z * NC + 1 - c) for z in range(NZ) for c in range(NC)]
    return lax.ppermute(value, "prow", pairs)


def split(value):
    high = value.astype(jnp.bfloat16)
    low = (value - high.astype(jnp.float32)).astype(jnp.bfloat16)
    return high, low


def near(value):
    return pltpu.with_memory_space_constraint(value, pltpu.VMEM)


def far(value):
    return pltpu.with_memory_space_constraint(value, pltpu.HBM)


def fast_call(kernel, shapes, operands, scalars, scratch, flops):
    return pl.pallas_call(
        kernel,
        in_specs=[pl.BlockSpec(memory_space=pltpu.SMEM)] * len(scalars)
        + [pl.BlockSpec(memory_space=pltpu.VMEM)] * len(operands),
        out_specs=[pl.BlockSpec(memory_space=pltpu.VMEM)] * len(shapes),
        out_shape=[pltpu.VMEM(shape, jnp.float32) for shape in shapes],
        scratch_shapes=scratch,
        compiler_params=pltpu.CompilerParams(vmem_limit_bytes=16 * 1024 * 1024),
        cost_estimate=pl.CostEstimate(flops=flops, bytes_accessed=4096, transcendentals=0),
    )(*scalars, *[near(value) for value in operands])


def pair_kernel(index, n_in, n_out, flip, has_init, waits, take, put, live, *refs):
    vectors, refs = refs[:n_in], refs[n_in:]
    blocks, refs = refs[0], refs[1:]
    init, refs = (refs[:n_out], refs[n_out:]) if has_init else ((), refs)
    refs = refs[waits:]
    outs, halves, total = refs[:n_out], refs[n_out], refs[n_out + 1]
    per = vectors[0].shape[0]
    for k in range(n_in):

        @pl.loop(0, per)
        def _(unit, k=k):
            high, low = split(vectors[k][unit])
            halves[k * per + unit, :W] = high
            halves[k * per + unit, W:] = low

    per = outs[0].shape[0]
    for k in range(n_out):

        @pl.loop(0, per)
        def _(unit, k=k):
            if has_init:
                total[k * per + unit] = init[k][unit]
            else:
                total[k * per + unit] = jnp.zeros((W, R), jnp.float32)

    @pl.loop(0, blocks.shape[1], step=UNROLL)
    def _(start):
        for j in range(UNROLL):
            slot = start + j
            block = jnp.where(live[slot] > 0, blocks[index, slot], 0.0)
            if flip:
                block = block.T
            high, low = split(block)
            left = jnp.concatenate(
                [jnp.concatenate([high, high], axis=1), jnp.concatenate([low, low], axis=1)], axis=0
            )
            product = jnp.dot(left, halves[take[slot]], preferred_element_type=jnp.float32)
            total[put[slot]] += product[:W] + product[W:]

    for k in range(n_out):

        @pl.loop(0, per)
        def _(unit, k=k):
            outs[k][unit] = total[k * per + unit]


def pair_product(index, flip, scalars, vectors, blocks, init, after, n_out, total):
    n_in = len(vectors)
    units = n_in * vectors[0].shape[0]
    return fast_call(
        functools.partial(pair_kernel, index, n_in, n_out, flip, init is not None, len(after)),
        [(total // n_out, W, R)] * n_out,
        [*vectors, blocks, *(init or ()), *after],
        scalars,
        [pltpu.VMEM((units, 2 * W, R), jnp.bfloat16), pltpu.VMEM((total, W, R), jnp.float32)],
        blocks.shape[1] * 8 * W * W * R,
    )


def dot(left, right):
    return jnp.dot(
        left, right, precision=lax.Precision.HIGHEST, preferred_element_type=jnp.float32
    )


def solve_kernel(level, flip, stacked, terms, inverse, base, *refs):
    value = base[level] if stacked else base[...]
    if terms:
        gone = refs[0][...]
        for ref in refs[1:terms]:
            gone = gone + ref[...]
        value = value - gone
    outs = refs[terms:]
    for flipped, out in zip(flip, outs):
        matrix = inverse[level]
        value = dot(matrix.T if flipped else matrix, value)
        out[...] = value


def solve(level, flip, inverse, base, gone):
    return fast_call(
        functools.partial(solve_kernel, level, flip, base.ndim == 3, len(gone)),
        [(W, R)] * len(flip),
        [inverse, base, *gone],
        [],
        [],
        12 * W * W * R,
    )


def add_kernel(terms, waits, *refs):
    for k, out in enumerate(refs[terms + waits :]):
        value = refs[0][k]
        for ref in refs[1:terms]:
            value = value + ref[k]
        out[...] = value


def add_units(parts, after):
    return fast_call(
        functools.partial(add_kernel, len(parts), len(after)),
        [(W, R)] * 4,
        [*parts, *after],
        [],
        [],
        len(parts) * 4 * W * R,
    )


def first_kernel(inverse, base, out, matrix, value, sems):
    copies = [
        pltpu.make_async_copy(inverse.at[0], matrix, sems.at[0]),
        pltpu.make_async_copy(base.at[0], value, sems.at[1]),
    ]
    for copy in copies:
        copy.start()
    for copy in copies:
        copy.wait()
    out[...] = dot(matrix[...], value[...])


def first_solve(inverse, base):
    return pl.pallas_call(
        first_kernel,
        in_specs=[pl.BlockSpec(memory_space=pl.ANY)] * 2,
        out_specs=pl.BlockSpec(memory_space=pltpu.VMEM),
        out_shape=pltpu.VMEM((W, R), jnp.float32),
        scratch_shapes=[
            pltpu.VMEM((W, W), jnp.float32),
            pltpu.VMEM((W, R), jnp.float32),
            pltpu.SemaphoreType.DMA((2,)),
        ],
        compiler_params=pltpu.CompilerParams(vmem_limit_bytes=16 * 1024 * 1024),
    )(far(inverse), far(base))


def load_kernel(blocks, after, out, sems):
    copies = [
        pltpu.make_async_copy(blocks.at[k], out.at[k], sems.at[k]) for k in range(blocks.shape[0])
    ]
    for copy in copies:
        copy.start()
    for copy in copies:
        copy.wait()


def load(blocks, after):
    return pl.pallas_call(
        load_kernel,
        in_specs=[pl.BlockSpec(memory_space=pl.ANY), pl.BlockSpec(memory_space=pltpu.VMEM)],
        out_specs=pl.BlockSpec(memory_space=pltpu.VMEM),
        out_shape=pltpu.VMEM(blocks.shape, jnp.float32),
        scratch_shapes=[pltpu.SemaphoreType.DMA((blocks.shape[0],))],
        compiler_params=pltpu.CompilerParams(vmem_limit_bytes=16 * 1024 * 1024),
        cost_estimate=pl.CostEstimate(
            flops=0, bytes_accessed=blocks.size * 4, transcendentals=0
        ),
    )(far(blocks), near(after))


def gather_plane(value):
    units = jnp.stack([value] + [shift_plane(value, d, 0) for d in PLAIN])
    return [units] + [shift_plane(units, d, 1) for d in PLAIN]


def scatter_plane(groups, beside):
    first = [shift_plane(groups[k], d, 0) for k, d in enumerate(FAR_FIRST, 1)]
    units = add_units([groups[0]] + first, beside(first[0]))
    return [units[0]] + [shift_plane(units[d], d, 1) for d in PLAIN]


def scatter_z(mine, other):
    units = add_units([mine, swap_core(other)], [])
    return [units[0]] + [shift_z(units[d], d) for d in PLAIN]


def gather_z(value):
    units = jnp.stack([value] + [shift_z(value, d) for d in PLAIN])
    return [units, swap_core(units)]


def place(offset, order):
    spot = jnp.zeros_like(offset)
    for k, d in enumerate(order, 1):
        spot = jnp.where(offset == d, k, spot)
    return spot


def body(rhs, dinv, blocks, targets, sources):
    right = rhs[:, 0, 0]
    inverse = dinv[:, 0, 0]
    aims = targets[0, 0]
    anchor = sources[0, 0]
    row = lax.axis_index("prow")
    col = lax.axis_index("pcol")
    z, core = row // NC, row % NC
    x, y = col // NY, col % NY
    live = (aims >= 0).astype(jnp.int32)
    rows = jnp.maximum(aims, 0)
    off_x = (x - anchor // NY) % NX
    off_y = (y - anchor % NY) % NY
    off_z = (z - rows // NC) % NZ
    first = core == 0
    to_x, to_y, to_z = (-off_x) % NX, (-off_y) % NY, (-off_z) % NZ
    take_plane = jnp.where(first, off_y * NX + off_x, off_x * NY + off_y)
    put_plane = jnp.where(
        first, place(to_x, FAR_FIRST) * NY + to_y, place(to_y, FAR_FIRST) * NX + to_x
    )
    across = (rows % NC != core).astype(jnp.int32) * NZ
    take_z = across + off_z
    put_z = across + to_z

    def forth(high, low, vectors, init):
        index = pair_index(high, low)
        scalars = (take_plane[index], put_z[index], live[index])
        return pair_product(index, False, scalars, vectors, panels, init, (), 2, 8)

    def back(high, low, vectors, init, after):
        index = pair_index(high, low)
        scalars = (take_z[index], put_plane[index], live[index])
        return pair_product(index, True, scalars, vectors, panels, init, after, 4, 16)

    top = LEV - 1
    solved = [None] * LEV
    result = [None] * LEV
    sums = [None] * LEV
    for level in range(LEV):
        gone = [] if level == 0 else scatter_z(*sums[level])
        if level == top:
            solved[level], result[level] = solve(level, (False, True), inverse, right, gone)
            break
        if level == 0:
            solved[level] = first_solve(inverse, right)
        else:
            (solved[level],) = solve(level, (False,), inverse, right, gone)
        vectors = gather_plane(solved[level])
        if level == 0:
            panels = load(blocks[0, 0], vectors[0])
        for high in range(level + 1, LEV):
            sums[high] = forth(high, level, vectors, sums[high])
    sums = [None] * LEV
    for level in reversed(range(1, LEV)):
        vectors = gather_z(result[level])

        def beside(held):
            done = []
            for low in reversed(range(level - 1)):
                sums[low] = back(level, low, vectors, sums[low], (held,))
                done += sums[low][:1]
            return done

        gone = scatter_plane(back(level, level - 1, vectors, sums[level - 1], ()), beside)
        (result[level - 1],) = solve(level - 1, (True,), inverse, solved[level - 1], gone)
    forward = jnp.stack(solved)[:, None, None]
    solution = jnp.stack(result)[:, None, None]
    return (forward, solution)


def solution(mesh):
    placed = (
        P(None, "prow", "pcol", None, None),
        P(None, "prow", "pcol", None, None),
        P("prow", "pcol", None, None, None, None),
        P("prow", "pcol", None, None),
        P("prow", "pcol", None, None),
    )
    return jax.shard_map(
        body,
        mesh=mesh,
        in_specs=placed,
        out_specs=(P(None, "prow", "pcol", None, None), P(None, "prow", "pcol", None, None)),
        check_vma=False,
    )
```

```python
import functools

import jax
import jax.numpy as jnp
from jax import lax
from jax.experimental import pallas as pl
from jax.experimental.pallas import tpu as pltpu
from jax.sharding import PartitionSpec as P

W = 128
R = 256
LEV = 4
NZ, NC, NX, NY = 4, 2, 4, 4
BOTH = ("prow", "pcol")
UNROLL = 16
ORDER = (2, 1, 3)


def pair_index(high, low):
    return high * (high - 1) // 2 + low


def device(z, c, x, y):
    return (z % NZ * NC + c) * NX * NY + x % NX * NY + y % NY


def shift_plane(value, step, phase):
    pairs = []
    for z in range(NZ):
        for c in range(NC):
            for x in range(NX):
                for y in range(NY):
                    if c == phase:
                        there = device(z, c, x + step, y)
                    else:
                        there = device(z, c, x, y + step)
                    pairs.append((device(z, c, x, y), there))
    return lax.ppermute(value, BOTH, pairs)


def shift_z(value, step):
    pairs = [(z * NC + c, (z + step) % NZ * NC + c) for z in range(NZ) for c in range(NC)]
    return lax.ppermute(value, "prow", pairs)


def swap_core(value):
    pairs = [(z * NC + c, z * NC + 1 - c) for z in range(NZ) for c in range(NC)]
    return lax.ppermute(value, "prow", pairs)


def split(value):
    high = value.astype(jnp.bfloat16)
    low = (value - high.astype(jnp.float32)).astype(jnp.bfloat16)
    return high, low


def near(value):
    return pltpu.with_memory_space_constraint(value, pltpu.VMEM)


def far(value):
    return pltpu.with_memory_space_constraint(value, pltpu.HBM)


def fast_call(kernel, shapes, operands, scalars, scratch, flops):
    return pl.pallas_call(
        kernel,
        in_specs=[pl.BlockSpec(memory_space=pltpu.SMEM)] * len(scalars)
        + [pl.BlockSpec(memory_space=pltpu.VMEM)] * len(operands),
        out_specs=[pl.BlockSpec(memory_space=pltpu.VMEM)] * len(shapes),
        out_shape=[pltpu.VMEM(shape, jnp.float32) for shape in shapes],
        scratch_shapes=scratch,
        compiler_params=pltpu.CompilerParams(vmem_limit_bytes=16 * 1024 * 1024),
        cost_estimate=pl.CostEstimate(flops=flops, bytes_accessed=4096, transcendentals=0),
    )(*scalars, *[near(value) for value in operands])


def pair_kernel(index, n_in, n_out, flip, has_init, waits, take, put, live, *refs):
    vectors, refs = refs[:n_in], refs[n_in:]
    blocks, refs = refs[0], refs[1:]
    init, refs = (refs[:n_out], refs[n_out:]) if has_init else ((), refs)
    refs = refs[waits:]
    outs, halves, total = refs[:n_out], refs[n_out], refs[n_out + 1]
    per = vectors[0].shape[0]
    for k in range(n_in):

        @pl.loop(0, per)
        def _(unit, k=k):
            high, low = split(vectors[k][unit])
            halves[k * per + unit, :W] = high
            halves[k * per + unit, W:] = low

    per = outs[0].shape[0]
    for k in range(n_out):

        @pl.loop(0, per)
        def _(unit, k=k):
            if has_init:
                total[k * per + unit] = init[k][unit]
            else:
                total[k * per + unit] = jnp.zeros((W, R), jnp.float32)

    @pl.loop(0, blocks.shape[1], step=UNROLL)
    def _(start):
        for j in range(UNROLL):
            slot = start + j
            block = jnp.where(live[slot] > 0, blocks[index, slot], 0.0)
            if flip:
                block = block.T
            high, low = split(block)
            left = jnp.concatenate(
                [jnp.concatenate([high, high], axis=1), jnp.concatenate([low, low], axis=1)], axis=0
            )
            product = jnp.dot(left, halves[take[slot]], preferred_element_type=jnp.float32)
            total[put[slot]] += product[:W] + product[W:]

    for k in range(n_out):

        @pl.loop(0, per)
        def _(unit, k=k):
            outs[k][unit] = total[k * per + unit]


def pair_product(index, flip, scalars, vectors, blocks, init, after, n_out, total):
    n_in = len(vectors)
    units = n_in * vectors[0].shape[0]
    return fast_call(
        functools.partial(pair_kernel, index, n_in, n_out, flip, init is not None, len(after)),
        [(total // n_out, W, R)] * n_out,
        [*vectors, blocks, *(init or ()), *after],
        scalars,
        [pltpu.VMEM((units, 2 * W, R), jnp.bfloat16), pltpu.VMEM((total, W, R), jnp.float32)],
        blocks.shape[1] * 8 * W * W * R,
    )


def dot(left, right):
    return jnp.dot(
        left, right, precision=lax.Precision.HIGHEST, preferred_element_type=jnp.float32
    )


def solve_kernel(level, flip, stacked, terms, inverse, base, *refs):
    value = base[level] if stacked else base[...]
    if terms:
        gone = refs[0][...]
        for ref in refs[1:terms]:
            gone = gone + ref[...]
        value = value - gone
    outs = refs[terms:]
    for flipped, out in zip(flip, outs):
        matrix = inverse[level]
        value = dot(matrix.T if flipped else matrix, value)
        out[...] = value


def solve(level, flip, inverse, base, gone):
    return fast_call(
        functools.partial(solve_kernel, level, flip, base.ndim == 3, len(gone)),
        [(W, R)] * len(flip),
        [inverse, base, *gone],
        [],
        [],
        12 * W * W * R,
    )


def add_kernel(terms, waits, *refs):
    for k, out in enumerate(refs[terms + waits :]):
        value = refs[0][k]
        for ref in refs[1:terms]:
            value = value + ref[k]
        out[...] = value


def add_units(parts, after):
    return fast_call(
        functools.partial(add_kernel, len(parts), len(after)),
        [(W, R)] * 4,
        [*parts, *after],
        [],
        [],
        len(parts) * 4 * W * R,
    )


def first_kernel(inverse, base, out, matrix, value, sems):
    copies = [
        pltpu.make_async_copy(inverse.at[0], matrix, sems.at[0]),
        pltpu.make_async_copy(base.at[0], value, sems.at[1]),
    ]
    for copy in copies:
        copy.start()
    for copy in copies:
        copy.wait()
    out[...] = dot(matrix[...], value[...])


def first_solve(inverse, base):
    return pl.pallas_call(
        first_kernel,
        in_specs=[pl.BlockSpec(memory_space=pl.ANY)] * 2,
        out_specs=pl.BlockSpec(memory_space=pltpu.VMEM),
        out_shape=pltpu.VMEM((W, R), jnp.float32),
        scratch_shapes=[
            pltpu.VMEM((W, W), jnp.float32),
            pltpu.VMEM((W, R), jnp.float32),
            pltpu.SemaphoreType.DMA((2,)),
        ],
        compiler_params=pltpu.CompilerParams(vmem_limit_bytes=16 * 1024 * 1024),
    )(far(inverse), far(base))


def load_kernel(blocks, after, out, sems):
    copies = [
        pltpu.make_async_copy(blocks.at[k], out.at[k], sems.at[k]) for k in range(blocks.shape[0])
    ]
    for copy in copies:
        copy.start()
    for copy in copies:
        copy.wait()


def load(blocks, after):
    return pl.pallas_call(
        load_kernel,
        in_specs=[pl.BlockSpec(memory_space=pl.ANY), pl.BlockSpec(memory_space=pltpu.VMEM)],
        out_specs=pl.BlockSpec(memory_space=pltpu.VMEM),
        out_shape=pltpu.VMEM(blocks.shape, jnp.float32),
        scratch_shapes=[pltpu.SemaphoreType.DMA((blocks.shape[0],))],
        compiler_params=pltpu.CompilerParams(vmem_limit_bytes=16 * 1024 * 1024),
        cost_estimate=pl.CostEstimate(
            flops=0, bytes_accessed=blocks.size * 4, transcendentals=0
        ),
    )(far(blocks), near(after))


def gather_plane(value):
    units = jnp.stack([value] + [shift_plane(value, d, 0) for d in ORDER])
    return [units] + [shift_plane(units, d, 1) for d in ORDER]


def scatter_plane(groups, beside):
    first = [shift_plane(groups[k], d, 0) for k, d in enumerate(ORDER, 1)]
    units = add_units([groups[0]] + first, beside(first[0]))
    return [units[0]] + [shift_plane(units[k], d, 1) for k, d in enumerate(ORDER, 1)]


def scatter_z(mine, other):
    units = add_units([mine, swap_core(other)], [])
    return [units[0]] + [shift_z(units[k], d) for k, d in enumerate(ORDER, 1)]


def gather_z(value):
    units = jnp.stack([value] + [shift_z(value, d) for d in ORDER])
    return [units, swap_core(units)]


def place(offset):
    spot = jnp.zeros_like(offset)
    for k, d in enumerate(ORDER, 1):
        spot = jnp.where(offset == d, k, spot)
    return spot


def body(rhs, dinv, blocks, targets, sources):
    right = rhs[:, 0, 0]
    inverse = dinv[:, 0, 0]
    aims = targets[0, 0]
    anchor = sources[0, 0]
    row = lax.axis_index("prow")
    col = lax.axis_index("pcol")
    z, core = row // NC, row % NC
    x, y = col // NY, col % NY
    live = (aims >= 0).astype(jnp.int32)
    rows = jnp.maximum(aims, 0)
    off_x = (x - anchor // NY) % NX
    off_y = (y - anchor % NY) % NY
    off_z = (z - rows // NC) % NZ
    first = core == 0
    from_x, from_y, from_z = [place(v) for v in (off_x, off_y, off_z)]
    to_x, to_y, to_z = [place((-v) % 4) for v in (off_x, off_y, off_z)]
    take_plane = jnp.where(first, from_y * NX + from_x, from_x * NY + from_y)
    put_plane = jnp.where(first, to_x * NY + to_y, to_y * NX + to_x)
    across = (rows % NC != core).astype(jnp.int32) * NZ
    take_z = across + from_z
    put_z = across + to_z

    def forth(high, low, vectors, init):
        index = pair_index(high, low)
        scalars = (take_plane[index], put_z[index], live[index])
        return pair_product(index, False, scalars, vectors, panels, init, (), 2, 8)

    def back(high, low, vectors, init, after):
        index = pair_index(high, low)
        scalars = (take_z[index], put_plane[index], live[index])
        return pair_product(index, True, scalars, vectors, panels, init, after, 4, 16)

    top = LEV - 1
    solved = [None] * LEV
    result = [None] * LEV
    sums = [None] * LEV
    for level in range(LEV):
        gone = [] if level == 0 else scatter_z(*sums[level])
        if level == top:
            solved[level], result[level] = solve(level, (False, True), inverse, right, gone)
            break
        if level == 0:
            solved[level] = first_solve(inverse, right)
        else:
            (solved[level],) = solve(level, (False,), inverse, right, gone)
        vectors = gather_plane(solved[level])
        if level == 0:
            panels = load(blocks[0, 0], vectors[0])
        for high in range(level + 1, LEV):
            sums[high] = forth(high, level, vectors, sums[high])
    sums = [None] * LEV
    for level in reversed(range(1, LEV)):
        vectors = gather_z(result[level])

        def beside(held):
            done = []
            for low in reversed(range(level - 1)):
                sums[low] = back(level, low, vectors, sums[low], (held,))
                done += sums[low][:1]
            return done

        gone = scatter_plane(back(level, level - 1, vectors, sums[level - 1], ()), beside)
        (result[level - 1],) = solve(level - 1, (True,), inverse, solved[level - 1], gone)
    forward = jnp.stack(solved)[:, None, None]
    solution = jnp.stack(result)[:, None, None]
    return (forward, solution)


def solution(mesh):
    placed = (
        P(None, "prow", "pcol", None, None),
        P(None, "prow", "pcol", None, None),
        P("prow", "pcol", None, None, None, None),
        P("prow", "pcol", None, None),
        P("prow", "pcol", None, None),
    )
    return jax.shard_map(
        body,
        mesh=mesh,
        in_specs=placed,
        out_specs=(P(None, "prow", "pcol", None, None), P(None, "prow", "pcol", None, None)),
        check_vma=False,
    )
```

```python
import functools

import jax
import jax.numpy as jnp
from jax import lax
from jax.experimental import pallas as pl
from jax.experimental.pallas import tpu as pltpu
from jax.sharding import PartitionSpec as P

W = 128
R = 256
LEV = 4
NZ, NC, NX, NY = 4, 2, 4, 4
BOTH = ("prow", "pcol")
WHOLE, SHORT = 32, 8
ORDER = (2, 1, 3)


def pair_index(high, low):
    return high * (high - 1) // 2 + low


def device(z, c, x, y):
    return (z % NZ * NC + c) * NX * NY + x % NX * NY + y % NY


def shift_plane(value, step, phase):
    pairs = []
    for z in range(NZ):
        for c in range(NC):
            for x in range(NX):
                for y in range(NY):
                    if c == phase:
                        there = device(z, c, x + step, y)
                    else:
                        there = device(z, c, x, y + step)
                    pairs.append((device(z, c, x, y), there))
    return lax.ppermute(value, BOTH, pairs)


def shift_z(value, step):
    pairs = [(z * NC + c, (z + step) % NZ * NC + c) for z in range(NZ) for c in range(NC)]
    return lax.ppermute(value, "prow", pairs)


def swap_core(value):
    pairs = [(z * NC + c, z * NC + 1 - c) for z in range(NZ) for c in range(NC)]
    return lax.ppermute(value, "prow", pairs)


def split(value):
    high = value.astype(jnp.bfloat16)
    low = (value - high.astype(jnp.float32)).astype(jnp.bfloat16)
    return high, low


def near(value):
    return pltpu.with_memory_space_constraint(value, pltpu.VMEM)


def far(value):
    return pltpu.with_memory_space_constraint(value, pltpu.HBM)


def fast_call(kernel, shapes, operands, scalars, scratch, flops):
    return pl.pallas_call(
        kernel,
        in_specs=[pl.BlockSpec(memory_space=pltpu.SMEM)] * len(scalars)
        + [pl.BlockSpec(memory_space=pltpu.VMEM)] * len(operands),
        out_specs=[pl.BlockSpec(memory_space=pltpu.VMEM)] * len(shapes),
        out_shape=[pltpu.VMEM(shape, jnp.float32) for shape in shapes],
        scratch_shapes=scratch,
        compiler_params=pltpu.CompilerParams(vmem_limit_bytes=16 * 1024 * 1024),
        cost_estimate=pl.CostEstimate(flops=flops, bytes_accessed=4096, transcendentals=0),
    )(*scalars, *[near(value) for value in operands])


def pair_kernel(index, unroll, n_in, n_out, flip, has_init, waits, take, put, live, *refs):
    vectors, refs = refs[:n_in], refs[n_in:]
    blocks, refs = refs[0], refs[1:]
    init, refs = (refs[:n_out], refs[n_out:]) if has_init else ((), refs)
    refs = refs[waits:]
    outs, halves, total = refs[:n_out], refs[n_out], refs[n_out + 1]
    per = vectors[0].shape[0]
    for k in range(n_in):

        @pl.loop(0, per)
        def _(unit, k=k):
            high, low = split(vectors[k][unit])
            halves[k * per + unit, :W] = high
            halves[k * per + unit, W:] = low

    per = outs[0].shape[0]
    for k in range(n_out):

        @pl.loop(0, per)
        def _(unit, k=k):
            if has_init:
                total[k * per + unit] = init[k][unit]
            else:
                total[k * per + unit] = jnp.zeros((W, R), jnp.float32)

    @pl.loop(0, blocks.shape[1], step=unroll)
    def _(start):
        for j in range(unroll):
            slot = start + j
            block = jnp.where(live[slot] > 0, blocks[index, slot], 0.0)
            if flip:
                block = block.T
            high, low = split(block)
            left = jnp.concatenate(
                [jnp.concatenate([high, high], axis=1), jnp.concatenate([low, low], axis=1)], axis=0
            )
            product = jnp.dot(left, halves[take[slot]], preferred_element_type=jnp.float32)
            total[put[slot]] += product[:W] + product[W:]

    for k in range(n_out):

        @pl.loop(0, per)
        def _(unit, k=k):
            outs[k][unit] = total[k * per + unit]


def pair_product(index, unroll, flip, scalars, vectors, blocks, init, after, n_out, total):
    n_in = len(vectors)
    units = n_in * vectors[0].shape[0]
    return fast_call(
        functools.partial(pair_kernel, index, unroll, n_in, n_out, flip, init is not None, len(after)),
        [(total // n_out, W, R)] * n_out,
        [*vectors, blocks, *(init or ()), *after],
        scalars,
        [pltpu.VMEM((units, 2 * W, R), jnp.bfloat16), pltpu.VMEM((total, W, R), jnp.float32)],
        blocks.shape[1] * 8 * W * W * R,
    )


def dot(left, right):
    return jnp.dot(
        left, right, precision=lax.Precision.HIGHEST, preferred_element_type=jnp.float32
    )


def solve_kernel(level, flip, stacked, terms, inverse, base, *refs):
    value = base[level] if stacked else base[...]
    if terms:
        gone = refs[0][...]
        for ref in refs[1:terms]:
            gone = gone + ref[...]
        value = value - gone
    outs = refs[terms:]
    for flipped, out in zip(flip, outs):
        matrix = inverse[level]
        value = dot(matrix.T if flipped else matrix, value)
        out[...] = value


def solve(level, flip, inverse, base, gone):
    return fast_call(
        functools.partial(solve_kernel, level, flip, base.ndim == 3, len(gone)),
        [(W, R)] * len(flip),
        [inverse, base, *gone],
        [],
        [],
        12 * W * W * R,
    )


def add_kernel(terms, waits, *refs):
    for k, out in enumerate(refs[terms + waits :]):
        value = refs[0][k]
        for ref in refs[1:terms]:
            value = value + ref[k]
        out[...] = value


def add_units(parts, after):
    return fast_call(
        functools.partial(add_kernel, len(parts), len(after)),
        [(W, R)] * 4,
        [*parts, *after],
        [],
        [],
        len(parts) * 4 * W * R,
    )


def first_kernel(inverse, base, out, matrix, value, sems):
    copies = [
        pltpu.make_async_copy(inverse.at[0], matrix, sems.at[0]),
        pltpu.make_async_copy(base.at[0], value, sems.at[1]),
    ]
    for copy in copies:
        copy.start()
    for copy in copies:
        copy.wait()
    out[...] = dot(matrix[...], value[...])


def first_solve(inverse, base):
    return pl.pallas_call(
        first_kernel,
        in_specs=[pl.BlockSpec(memory_space=pl.ANY)] * 2,
        out_specs=pl.BlockSpec(memory_space=pltpu.VMEM),
        out_shape=pltpu.VMEM((W, R), jnp.float32),
        scratch_shapes=[
            pltpu.VMEM((W, W), jnp.float32),
            pltpu.VMEM((W, R), jnp.float32),
            pltpu.SemaphoreType.DMA((2,)),
        ],
        compiler_params=pltpu.CompilerParams(vmem_limit_bytes=16 * 1024 * 1024),
    )(far(inverse), far(base))


def load_kernel(blocks, after, out, sems):
    copies = [
        pltpu.make_async_copy(blocks.at[k], out.at[k], sems.at[k]) for k in range(blocks.shape[0])
    ]
    for copy in copies:
        copy.start()
    for copy in copies:
        copy.wait()


def load(blocks, after):
    return pl.pallas_call(
        load_kernel,
        in_specs=[pl.BlockSpec(memory_space=pl.ANY), pl.BlockSpec(memory_space=pltpu.VMEM)],
        out_specs=pl.BlockSpec(memory_space=pltpu.VMEM),
        out_shape=pltpu.VMEM(blocks.shape, jnp.float32),
        scratch_shapes=[pltpu.SemaphoreType.DMA((blocks.shape[0],))],
        compiler_params=pltpu.CompilerParams(vmem_limit_bytes=16 * 1024 * 1024),
        cost_estimate=pl.CostEstimate(
            flops=0, bytes_accessed=blocks.size * 4, transcendentals=0
        ),
    )(far(blocks), near(after))


def gather_plane(value):
    units = jnp.stack([value] + [shift_plane(value, d, 0) for d in ORDER])
    return [units] + [shift_plane(units, d, 1) for d in ORDER]


def scatter_plane(groups, beside):
    first = [shift_plane(groups[k], d, 0) for k, d in enumerate(ORDER, 1)]
    units = add_units([groups[0]] + first, beside(first[0]))
    return [units[0]] + [shift_plane(units[k], d, 1) for k, d in enumerate(ORDER, 1)]


def scatter_z(mine, other):
    units = add_units([mine, swap_core(other)], [])
    return [units[0]] + [shift_z(units[k], d) for k, d in enumerate(ORDER, 1)]


def gather_z(value):
    units = jnp.stack([value] + [shift_z(value, d) for d in ORDER])
    return [units, swap_core(units)]


def place(offset):
    spot = jnp.zeros_like(offset)
    for k, d in enumerate(ORDER, 1):
        spot = jnp.where(offset == d, k, spot)
    return spot


def body(rhs, dinv, blocks, targets, sources):
    right = rhs[:, 0, 0]
    inverse = dinv[:, 0, 0]
    aims = targets[0, 0]
    anchor = sources[0, 0]
    row = lax.axis_index("prow")
    col = lax.axis_index("pcol")
    z, core = row // NC, row % NC
    x, y = col // NY, col % NY
    live = (aims >= 0).astype(jnp.int32)
    rows = jnp.maximum(aims, 0)
    off_x = (x - anchor // NY) % NX
    off_y = (y - anchor % NY) % NY
    off_z = (z - rows // NC) % NZ
    first = core == 0
    from_x, from_y, from_z = [place(v) for v in (off_x, off_y, off_z)]
    to_x, to_y, to_z = [place((-v) % 4) for v in (off_x, off_y, off_z)]
    take_plane = jnp.where(first, from_y * NX + from_x, from_x * NY + from_y)
    put_plane = jnp.where(first, to_x * NY + to_y, to_y * NX + to_x)
    across = (rows % NC != core).astype(jnp.int32) * NZ
    take_z = across + from_z
    put_z = across + to_z

    def forth(high, low, vectors, init):
        index = pair_index(high, low)
        scalars = (take_plane[index], put_z[index], live[index])
        unroll = WHOLE if high == low + 1 else SHORT
        return pair_product(index, unroll, False, scalars, vectors, panels, init, (), 2, 8)

    def back(high, low, vectors, init, after):
        index = pair_index(high, low)
        scalars = (take_z[index], put_plane[index], live[index])
        unroll = WHOLE if high == low + 1 else SHORT
        return pair_product(index, unroll, True, scalars, vectors, panels, init, after, 4, 16)

    top = LEV - 1
    solved = [None] * LEV
    result = [None] * LEV
    sums = [None] * LEV
    for level in range(LEV):
        gone = [] if level == 0 else scatter_z(*sums[level])
        if level == top:
            solved[level], result[level] = solve(level, (False, True), inverse, right, gone)
            break
        if level == 0:
            solved[level] = first_solve(inverse, right)
        else:
            (solved[level],) = solve(level, (False,), inverse, right, gone)
        vectors = gather_plane(solved[level])
        if level == 0:
            panels = load(blocks[0, 0], vectors[0])
        for high in range(level + 1, LEV):
            sums[high] = forth(high, level, vectors, sums[high])
    sums = [None] * LEV
    for level in reversed(range(1, LEV)):
        vectors = gather_z(result[level])

        def beside(held):
            done = []
            for low in reversed(range(level - 1)):
                sums[low] = back(level, low, vectors, sums[low], (held,))
                done += sums[low][:1]
            return done

        gone = scatter_plane(back(level, level - 1, vectors, sums[level - 1], ()), beside)
        (result[level - 1],) = solve(level - 1, (True,), inverse, solved[level - 1], gone)
    forward = jnp.stack(solved)[:, None, None]
    solution = jnp.stack(result)[:, None, None]
    return (forward, solution)


def solution(mesh):
    placed = (
        P(None, "prow", "pcol", None, None),
        P(None, "prow", "pcol", None, None),
        P("prow", "pcol", None, None, None, None),
        P("prow", "pcol", None, None),
        P("prow", "pcol", None, None),
    )
    return jax.shard_map(
        body,
        mesh=mesh,
        in_specs=placed,
        out_specs=(P(None, "prow", "pcol", None, None), P(None, "prow", "pcol", None, None)),
        check_vma=False,
    )
```

```python
import functools

import jax
import jax.numpy as jnp
from jax import lax
from jax.experimental import pallas as pl
from jax.experimental.pallas import tpu as pltpu
from jax.sharding import PartitionSpec as P

W = 128
R = 256
LEV = 4
NZ, NC, NX, NY = 4, 2, 4, 4
BOTH = ("prow", "pcol")
WHOLE, HALF, SHORT = 32, 16, 8
ORDER = (2, 1, 3)


def pair_index(high, low):
    return high * (high - 1) // 2 + low


def device(z, c, x, y):
    return (z % NZ * NC + c) * NX * NY + x % NX * NY + y % NY


def shift_plane(value, step, phase):
    pairs = []
    for z in range(NZ):
        for c in range(NC):
            for x in range(NX):
                for y in range(NY):
                    if c == phase:
                        there = device(z, c, x + step, y)
                    else:
                        there = device(z, c, x, y + step)
                    pairs.append((device(z, c, x, y), there))
    return lax.ppermute(value, BOTH, pairs)


def shift_z(value, step):
    pairs = [(z * NC + c, (z + step) % NZ * NC + c) for z in range(NZ) for c in range(NC)]
    return lax.ppermute(value, "prow", pairs)


def swap_core(value):
    pairs = [(z * NC + c, z * NC + 1 - c) for z in range(NZ) for c in range(NC)]
    return lax.ppermute(value, "prow", pairs)


def split(value):
    high = value.astype(jnp.bfloat16)
    low = (value - high.astype(jnp.float32)).astype(jnp.bfloat16)
    return high, low


def near(value):
    return pltpu.with_memory_space_constraint(value, pltpu.VMEM)


def far(value):
    return pltpu.with_memory_space_constraint(value, pltpu.HBM)


def fast_call(kernel, shapes, operands, scalars, scratch, flops):
    return pl.pallas_call(
        kernel,
        in_specs=[pl.BlockSpec(memory_space=pltpu.SMEM)] * len(scalars)
        + [pl.BlockSpec(memory_space=pltpu.VMEM)] * len(operands),
        out_specs=[pl.BlockSpec(memory_space=pltpu.VMEM)] * len(shapes),
        out_shape=[pltpu.VMEM(shape, jnp.float32) for shape in shapes],
        scratch_shapes=scratch,
        compiler_params=pltpu.CompilerParams(vmem_limit_bytes=16 * 1024 * 1024),
        cost_estimate=pl.CostEstimate(flops=flops, bytes_accessed=4096, transcendentals=0),
    )(*scalars, *[near(value) for value in operands])


def pair_kernel(index, unroll, n_in, n_out, flip, has_init, waits, take, put, live, *refs):
    vectors, refs = refs[:n_in], refs[n_in:]
    blocks, refs = refs[0], refs[1:]
    init, refs = (refs[:n_out], refs[n_out:]) if has_init else ((), refs)
    refs = refs[waits:]
    outs, halves, total = refs[:n_out], refs[n_out], refs[n_out + 1]
    per = vectors[0].shape[0]
    for k in range(n_in):

        @pl.loop(0, per)
        def _(unit, k=k):
            high, low = split(vectors[k][unit])
            halves[k * per + unit, :W] = high
            halves[k * per + unit, W:] = low

    per = outs[0].shape[0]
    for k in range(n_out):

        @pl.loop(0, per)
        def _(unit, k=k):
            if has_init:
                total[k * per + unit] = init[k][unit]
            else:
                total[k * per + unit] = jnp.zeros((W, R), jnp.float32)

    @pl.loop(0, blocks.shape[1], step=unroll)
    def _(start):
        for j in range(unroll):
            slot = start + j
            block = jnp.where(live[slot] > 0, blocks[index, slot], 0.0)
            if flip:
                block = block.T
            high, low = split(block)
            left = jnp.concatenate(
                [jnp.concatenate([high, high], axis=1), jnp.concatenate([low, low], axis=1)], axis=0
            )
            product = jnp.dot(left, halves[take[slot]], preferred_element_type=jnp.float32)
            total[put[slot]] += product[:W] + product[W:]

    for k in range(n_out):

        @pl.loop(0, per)
        def _(unit, k=k):
            outs[k][unit] = total[k * per + unit]


def pair_product(index, unroll, flip, scalars, vectors, blocks, init, after, n_out, total):
    n_in = len(vectors)
    units = n_in * vectors[0].shape[0]
    return fast_call(
        functools.partial(pair_kernel, index, unroll, n_in, n_out, flip, init is not None, len(after)),
        [(total // n_out, W, R)] * n_out,
        [*vectors, blocks, *(init or ()), *after],
        scalars,
        [pltpu.VMEM((units, 2 * W, R), jnp.bfloat16), pltpu.VMEM((total, W, R), jnp.float32)],
        blocks.shape[1] * 8 * W * W * R,
    )


def dot(left, right):
    return jnp.dot(
        left, right, precision=lax.Precision.HIGHEST, preferred_element_type=jnp.float32
    )


def solve_kernel(level, flip, stacked, terms, inverse, base, *refs):
    value = base[level] if stacked else base[...]
    if terms:
        gone = refs[0][...]
        for ref in refs[1:terms]:
            gone = gone + ref[...]
        value = value - gone
    outs = refs[terms:]
    for flipped, out in zip(flip, outs):
        matrix = inverse[level]
        value = dot(matrix.T if flipped else matrix, value)
        out[...] = value


def solve(level, flip, inverse, base, gone):
    return fast_call(
        functools.partial(solve_kernel, level, flip, base.ndim == 3, len(gone)),
        [(W, R)] * len(flip),
        [inverse, base, *gone],
        [],
        [],
        12 * W * W * R,
    )


def add_kernel(terms, waits, *refs):
    for k, out in enumerate(refs[terms + waits :]):
        value = refs[0][k]
        for ref in refs[1:terms]:
            value = value + ref[k]
        out[...] = value


def add_units(parts, after):
    return fast_call(
        functools.partial(add_kernel, len(parts), len(after)),
        [(W, R)] * 4,
        [*parts, *after],
        [],
        [],
        len(parts) * 4 * W * R,
    )


def first_kernel(inverse, base, out, matrix, value, sems):
    copies = [
        pltpu.make_async_copy(inverse.at[0], matrix, sems.at[0]),
        pltpu.make_async_copy(base.at[0], value, sems.at[1]),
    ]
    for copy in copies:
        copy.start()
    for copy in copies:
        copy.wait()
    out[...] = dot(matrix[...], value[...])


def first_solve(inverse, base):
    return pl.pallas_call(
        first_kernel,
        in_specs=[pl.BlockSpec(memory_space=pl.ANY)] * 2,
        out_specs=pl.BlockSpec(memory_space=pltpu.VMEM),
        out_shape=pltpu.VMEM((W, R), jnp.float32),
        scratch_shapes=[
            pltpu.VMEM((W, W), jnp.float32),
            pltpu.VMEM((W, R), jnp.float32),
            pltpu.SemaphoreType.DMA((2,)),
        ],
        compiler_params=pltpu.CompilerParams(vmem_limit_bytes=16 * 1024 * 1024),
    )(far(inverse), far(base))


def load_kernel(blocks, after, out, sems):
    copies = [
        pltpu.make_async_copy(blocks.at[k], out.at[k], sems.at[k]) for k in range(blocks.shape[0])
    ]
    for copy in copies:
        copy.start()
    for copy in copies:
        copy.wait()


def load(blocks, after):
    return pl.pallas_call(
        load_kernel,
        in_specs=[pl.BlockSpec(memory_space=pl.ANY), pl.BlockSpec(memory_space=pltpu.VMEM)],
        out_specs=pl.BlockSpec(memory_space=pltpu.VMEM),
        out_shape=pltpu.VMEM(blocks.shape, jnp.float32),
        scratch_shapes=[pltpu.SemaphoreType.DMA((blocks.shape[0],))],
        compiler_params=pltpu.CompilerParams(vmem_limit_bytes=16 * 1024 * 1024),
        cost_estimate=pl.CostEstimate(
            flops=0, bytes_accessed=blocks.size * 4, transcendentals=0
        ),
    )(far(blocks), near(after))


def gather_plane(value):
    units = jnp.stack([value] + [shift_plane(value, d, 0) for d in ORDER])
    return [units] + [shift_plane(units, d, 1) for d in ORDER]


def scatter_plane(groups, beside):
    first = [shift_plane(groups[k], d, 0) for k, d in enumerate(ORDER, 1)]
    units = add_units([groups[0]] + first, beside(first[0]))
    return [units[0]] + [shift_plane(units[k], d, 1) for k, d in enumerate(ORDER, 1)]


def scatter_z(mine, other):
    units = add_units([mine, swap_core(other)], [])
    return [units[0]] + [shift_z(units[k], d) for k, d in enumerate(ORDER, 1)]


def gather_z(value):
    units = jnp.stack([value] + [shift_z(value, d) for d in ORDER])
    return [units, swap_core(units)]


def place(offset):
    spot = jnp.zeros_like(offset)
    for k, d in enumerate(ORDER, 1):
        spot = jnp.where(offset == d, k, spot)
    return spot


def body(rhs, dinv, blocks, targets, sources):
    right = rhs[:, 0, 0]
    inverse = dinv[:, 0, 0]
    aims = targets[0, 0]
    anchor = sources[0, 0]
    row = lax.axis_index("prow")
    col = lax.axis_index("pcol")
    z, core = row // NC, row % NC
    x, y = col // NY, col % NY
    live = (aims >= 0).astype(jnp.int32)
    rows = jnp.maximum(aims, 0)
    off_x = (x - anchor // NY) % NX
    off_y = (y - anchor % NY) % NY
    off_z = (z - rows // NC) % NZ
    first = core == 0
    from_x, from_y, from_z = [place(v) for v in (off_x, off_y, off_z)]
    to_x, to_y, to_z = [place((-v) % 4) for v in (off_x, off_y, off_z)]
    take_plane = jnp.where(first, from_y * NX + from_x, from_x * NY + from_y)
    put_plane = jnp.where(first, to_x * NY + to_y, to_y * NX + to_x)
    across = (rows % NC != core).astype(jnp.int32) * NZ
    take_z = across + from_z
    put_z = across + to_z

    def forth(high, low, vectors, init):
        index = pair_index(high, low)
        scalars = (take_plane[index], put_z[index], live[index])
        unroll = WHOLE if high == low + 1 else SHORT
        return pair_product(index, unroll, False, scalars, vectors, panels, init, (), 2, 8)

    def back(high, low, vectors, init, after):
        index = pair_index(high, low)
        scalars = (take_z[index], put_plane[index], live[index])
        unroll = WHOLE if high == low + 1 else HALF if high == LEV - 1 else SHORT
        return pair_product(index, unroll, True, scalars, vectors, panels, init, after, 4, 16)

    top = LEV - 1
    solved = [None] * LEV
    result = [None] * LEV
    sums = [None] * LEV
    for level in range(LEV):
        gone = [] if level == 0 else scatter_z(*sums[level])
        if level == top:
            solved[level], result[level] = solve(level, (False, True), inverse, right, gone)
            break
        if level == 0:
            solved[level] = first_solve(inverse, right)
        else:
            (solved[level],) = solve(level, (False,), inverse, right, gone)
        vectors = gather_plane(solved[level])
        if level == 0:
            panels = load(blocks[0, 0], vectors[0])
        for high in range(level + 1, LEV):
            sums[high] = forth(high, level, vectors, sums[high])
    sums = [None] * LEV
    for level in reversed(range(1, LEV)):
        vectors = gather_z(result[level])

        def beside(held):
            done = []
            for low in reversed(range(level - 1)):
                sums[low] = back(level, low, vectors, sums[low], (held,))
                done += sums[low][:1]
            return done

        gone = scatter_plane(back(level, level - 1, vectors, sums[level - 1], ()), beside)
        (result[level - 1],) = solve(level - 1, (True,), inverse, solved[level - 1], gone)
    forward = jnp.stack(solved)[:, None, None]
    solution = jnp.stack(result)[:, None, None]
    return (forward, solution)


def solution(mesh):
    placed = (
        P(None, "prow", "pcol", None, None),
        P(None, "prow", "pcol", None, None),
        P("prow", "pcol", None, None, None, None),
        P("prow", "pcol", None, None),
        P("prow", "pcol", None, None),
    )
    return jax.shard_map(
        body,
        mesh=mesh,
        in_specs=placed,
        out_specs=(P(None, "prow", "pcol", None, None), P(None, "prow", "pcol", None, None)),
        check_vma=False,
    )
```

```python
import functools

import jax
import jax.numpy as jnp
from jax import lax
from jax.experimental import pallas as pl
from jax.experimental.pallas import tpu as pltpu
from jax.sharding import PartitionSpec as P

W = 128
R = 256
LEV = 4
NZ, NC, NX, NY = 4, 2, 4, 4
BOTH = ("prow", "pcol")
WHOLE, HALF, SHORT = 32, 16, 8
ORDER = (2, 1, 3)


def pair_index(high, low):
    return high * (high - 1) // 2 + low


def device(z, c, x, y):
    return (z % NZ * NC + c) * NX * NY + x % NX * NY + y % NY


def shift_plane(value, step, phase):
    pairs = []
    for z in range(NZ):
        for c in range(NC):
            for x in range(NX):
                for y in range(NY):
                    if c == phase:
                        there = device(z, c, x + step, y)
                    else:
                        there = device(z, c, x, y + step)
                    pairs.append((device(z, c, x, y), there))
    return lax.ppermute(value, BOTH, pairs)


def shift_z(value, step):
    pairs = [(z * NC + c, (z + step) % NZ * NC + c) for z in range(NZ) for c in range(NC)]
    return lax.ppermute(value, "prow", pairs)


def swap_core(value):
    pairs = [(z * NC + c, z * NC + 1 - c) for z in range(NZ) for c in range(NC)]
    return lax.ppermute(value, "prow", pairs)


def split(value):
    high = value.astype(jnp.bfloat16)
    low = (value - high.astype(jnp.float32)).astype(jnp.bfloat16)
    return high, low


def near(value):
    return pltpu.with_memory_space_constraint(value, pltpu.VMEM)


def far(value):
    return pltpu.with_memory_space_constraint(value, pltpu.HBM)


def fast_call(kernel, shapes, operands, scalars, scratch, flops):
    return pl.pallas_call(
        kernel,
        in_specs=[pl.BlockSpec(memory_space=pltpu.SMEM)] * len(scalars)
        + [pl.BlockSpec(memory_space=pltpu.VMEM)] * len(operands),
        out_specs=[pl.BlockSpec(memory_space=pltpu.VMEM)] * len(shapes),
        out_shape=[pltpu.VMEM(shape, jnp.float32) for shape in shapes],
        scratch_shapes=scratch,
        compiler_params=pltpu.CompilerParams(vmem_limit_bytes=16 * 1024 * 1024),
        cost_estimate=pl.CostEstimate(flops=flops, bytes_accessed=4096, transcendentals=0),
    )(*scalars, *[near(value) for value in operands])


def pair_kernel(index, unroll, n_in, n_out, flip, has_init, waits, take, put, live, *refs):
    vectors, refs = refs[:n_in], refs[n_in:]
    blocks, refs = refs[0], refs[1:]
    init, refs = (refs[:n_out], refs[n_out:]) if has_init else ((), refs)
    refs = refs[waits:]
    outs, halves, total = refs[:n_out], refs[n_out], refs[n_out + 1]
    per = vectors[0].shape[0]
    for k in range(n_in):

        @pl.loop(0, per)
        def _(unit, k=k):
            high, low = split(vectors[k][unit])
            halves[k * per + unit, :W] = high
            halves[k * per + unit, W:] = low

    per = outs[0].shape[0]
    for k in range(n_out):

        @pl.loop(0, per)
        def _(unit, k=k):
            if has_init:
                total[k * per + unit] = init[k][unit]
            else:
                total[k * per + unit] = jnp.zeros((W, R), jnp.float32)

    @pl.loop(0, blocks.shape[1], step=unroll)
    def _(start):
        for j in range(unroll):
            slot = start + j
            block = jnp.where(live[slot] > 0, blocks[index, slot], 0.0)
            if flip:
                block = block.T
            high, low = split(block)
            left = jnp.concatenate(
                [jnp.concatenate([high, high], axis=1), jnp.concatenate([low, low], axis=1)], axis=0
            )
            product = jnp.dot(left, halves[take[slot]], preferred_element_type=jnp.float32)
            total[put[slot]] += product[:W] + product[W:]

    for k in range(n_out):

        @pl.loop(0, per)
        def _(unit, k=k):
            outs[k][unit] = total[k * per + unit]


def pair_product(index, unroll, flip, scalars, vectors, blocks, init, after, n_out, total):
    n_in = len(vectors)
    units = n_in * vectors[0].shape[0]
    return fast_call(
        functools.partial(pair_kernel, index, unroll, n_in, n_out, flip, init is not None, len(after)),
        [(total // n_out, W, R)] * n_out,
        [*vectors, blocks, *(init or ()), *after],
        scalars,
        [pltpu.VMEM((units, 2 * W, R), jnp.bfloat16), pltpu.VMEM((total, W, R), jnp.float32)],
        blocks.shape[1] * 8 * W * W * R,
    )


def dot(left, right):
    return jnp.dot(
        left, right, precision=lax.Precision.HIGHEST, preferred_element_type=jnp.float32
    )


def solve_kernel(level, flip, stacked, terms, inverse, base, *refs):
    value = base[level] if stacked else base[...]
    if terms:
        gone = refs[0][...]
        for ref in refs[1:terms]:
            gone = gone + ref[...]
        value = value - gone
    outs = refs[terms:]
    for flipped, out in zip(flip, outs):
        matrix = inverse[level]
        value = dot(matrix.T if flipped else matrix, value)
        out[...] = value


def solve(level, flip, inverse, base, gone):
    return fast_call(
        functools.partial(solve_kernel, level, flip, base.ndim == 3, len(gone)),
        [(W, R)] * len(flip),
        [inverse, base, *gone],
        [],
        [],
        12 * W * W * R,
    )


def add_kernel(terms, waits, *refs):
    for k, out in enumerate(refs[terms + waits :]):
        value = refs[0][k]
        for ref in refs[1:terms]:
            value = value + ref[k]
        out[...] = value


def add_units(parts, after):
    return fast_call(
        functools.partial(add_kernel, len(parts), len(after)),
        [(W, R)] * 4,
        [*parts, *after],
        [],
        [],
        len(parts) * 4 * W * R,
    )


def first_kernel(inverse, base, out, matrix, value, sems):
    copies = [
        pltpu.make_async_copy(inverse.at[0], matrix, sems.at[0]),
        pltpu.make_async_copy(base.at[0], value, sems.at[1]),
    ]
    for copy in copies:
        copy.start()
    for copy in copies:
        copy.wait()
    out[...] = dot(matrix[...], value[...])


def first_solve(inverse, base):
    return pl.pallas_call(
        first_kernel,
        in_specs=[pl.BlockSpec(memory_space=pl.ANY)] * 2,
        out_specs=pl.BlockSpec(memory_space=pltpu.VMEM),
        out_shape=pltpu.VMEM((W, R), jnp.float32),
        scratch_shapes=[
            pltpu.VMEM((W, W), jnp.float32),
            pltpu.VMEM((W, R), jnp.float32),
            pltpu.SemaphoreType.DMA((2,)),
        ],
        compiler_params=pltpu.CompilerParams(vmem_limit_bytes=16 * 1024 * 1024),
    )(far(inverse), far(base))


def last_kernel(inverse, base, *refs):
    gone, done, (out, value, sems) = refs[:4], refs[4 : 3 + LEV], refs[3 + LEV :]
    copies = [
        pltpu.make_async_copy(ref, out.at[k], sems.at[k]) for k, ref in enumerate(done, 1)
    ]
    for copy in copies:
        copy.start()
    update = gone[0][...] + gone[1][...] + gone[2][...] + gone[3][...]
    value[...] = dot(inverse[0].T, base[...] - update)
    copies.append(pltpu.make_async_copy(value, out.at[0], sems.at[0]))
    copies[-1].start()
    for copy in copies:
        copy.wait()


def last_solve(inverse, base, gone, done):
    operands = [inverse, base, *gone, *done]
    return pl.pallas_call(
        last_kernel,
        in_specs=[pl.BlockSpec(memory_space=pltpu.VMEM)] * len(operands),
        out_specs=pl.BlockSpec(memory_space=pl.ANY),
        out_shape=pltpu.HBM((LEV, W, R), jnp.float32),
        scratch_shapes=[pltpu.VMEM((W, R), jnp.float32), pltpu.SemaphoreType.DMA((LEV,))],
        compiler_params=pltpu.CompilerParams(vmem_limit_bytes=16 * 1024 * 1024),
        cost_estimate=pl.CostEstimate(flops=12 * W * W * R, bytes_accessed=4096, transcendentals=0),
    )(*[near(value) for value in operands])


def load_kernel(blocks, after, out, sems):
    copies = [
        pltpu.make_async_copy(blocks.at[k], out.at[k], sems.at[k]) for k in range(blocks.shape[0])
    ]
    for copy in copies:
        copy.start()
    for copy in copies:
        copy.wait()


def load(blocks, after):
    return pl.pallas_call(
        load_kernel,
        in_specs=[pl.BlockSpec(memory_space=pl.ANY), pl.BlockSpec(memory_space=pltpu.VMEM)],
        out_specs=pl.BlockSpec(memory_space=pltpu.VMEM),
        out_shape=pltpu.VMEM(blocks.shape, jnp.float32),
        scratch_shapes=[pltpu.SemaphoreType.DMA((blocks.shape[0],))],
        compiler_params=pltpu.CompilerParams(vmem_limit_bytes=16 * 1024 * 1024),
        cost_estimate=pl.CostEstimate(
            flops=0, bytes_accessed=blocks.size * 4, transcendentals=0
        ),
    )(far(blocks), near(after))


def gather_plane(value):
    units = jnp.stack([value] + [shift_plane(value, d, 0) for d in ORDER])
    return [units] + [shift_plane(units, d, 1) for d in ORDER]


def scatter_plane(groups, beside):
    first = [shift_plane(groups[k], d, 0) for k, d in enumerate(ORDER, 1)]
    units = add_units([groups[0]] + first, beside(first[0]))
    return [units[0]] + [shift_plane(units[k], d, 1) for k, d in enumerate(ORDER, 1)]


def scatter_z(mine, other):
    units = add_units([mine, swap_core(other)], [])
    return [units[0]] + [shift_z(units[k], d) for k, d in enumerate(ORDER, 1)]


def gather_z(value):
    units = jnp.stack([value] + [shift_z(value, d) for d in ORDER])
    return [units, swap_core(units)]


def place(offset):
    spot = jnp.zeros_like(offset)
    for k, d in enumerate(ORDER, 1):
        spot = jnp.where(offset == d, k, spot)
    return spot


def body(rhs, dinv, blocks, targets, sources):
    right = rhs[:, 0, 0]
    inverse = dinv[:, 0, 0]
    aims = targets[0, 0]
    anchor = sources[0, 0]
    row = lax.axis_index("prow")
    col = lax.axis_index("pcol")
    z, core = row // NC, row % NC
    x, y = col // NY, col % NY
    live = (aims >= 0).astype(jnp.int32)
    rows = jnp.maximum(aims, 0)
    off_x = (x - anchor // NY) % NX
    off_y = (y - anchor % NY) % NY
    off_z = (z - rows // NC) % NZ
    first = core == 0
    from_x, from_y, from_z = [place(v) for v in (off_x, off_y, off_z)]
    to_x, to_y, to_z = [place((-v) % 4) for v in (off_x, off_y, off_z)]
    take_plane = jnp.where(first, from_y * NX + from_x, from_x * NY + from_y)
    put_plane = jnp.where(first, to_x * NY + to_y, to_y * NX + to_x)
    across = (rows % NC != core).astype(jnp.int32) * NZ
    take_z = across + from_z
    put_z = across + to_z

    def forth(high, low, vectors, init):
        index = pair_index(high, low)
        scalars = (take_plane[index], put_z[index], live[index])
        unroll = WHOLE if high == low + 1 else SHORT
        return pair_product(index, unroll, False, scalars, vectors, panels, init, (), 2, 8)

    def back(high, low, vectors, init, after):
        index = pair_index(high, low)
        scalars = (take_z[index], put_plane[index], live[index])
        unroll = WHOLE if high == low + 1 else HALF if high == LEV - 1 else SHORT
        return pair_product(index, unroll, True, scalars, vectors, panels, init, after, 4, 16)

    top = LEV - 1
    solved = [None] * LEV
    result = [None] * LEV
    sums = [None] * LEV
    for level in range(LEV):
        gone = [] if level == 0 else scatter_z(*sums[level])
        if level == top:
            solved[level], result[level] = solve(level, (False, True), inverse, right, gone)
            break
        if level == 0:
            solved[level] = first_solve(inverse, right)
        else:
            (solved[level],) = solve(level, (False,), inverse, right, gone)
        vectors = gather_plane(solved[level])
        if level == 0:
            panels = load(blocks[0, 0], vectors[0])
        for high in range(level + 1, LEV):
            sums[high] = forth(high, level, vectors, sums[high])
    sums = [None] * LEV
    for level in reversed(range(1, LEV)):
        vectors = gather_z(result[level])

        def beside(held):
            done = []
            for low in reversed(range(level - 1)):
                sums[low] = back(level, low, vectors, sums[low], (held,))
                done += sums[low][:1]
            return done

        gone = scatter_plane(back(level, level - 1, vectors, sums[level - 1], ()), beside)
        if level > 1:
            (result[level - 1],) = solve(level - 1, (True,), inverse, solved[level - 1], gone)
    stacked = last_solve(inverse, solved[0], gone, result[1:])
    forward = jnp.stack(solved)[:, None, None]
    solution = stacked[:, None, None]
    return (forward, solution)


def solution(mesh):
    placed = (
        P(None, "prow", "pcol", None, None),
        P(None, "prow", "pcol", None, None),
        P("prow", "pcol", None, None, None, None),
        P("prow", "pcol", None, None),
        P("prow", "pcol", None, None),
    )
    return jax.shard_map(
        body,
        mesh=mesh,
        in_specs=placed,
        out_specs=(P(None, "prow", "pcol", None, None), P(None, "prow", "pcol", None, None)),
        check_vma=False,
    )
```

```python
import functools

import jax
import jax.numpy as jnp
from jax import lax
from jax.experimental import pallas as pl
from jax.experimental.pallas import tpu as pltpu
from jax.sharding import PartitionSpec as P

W = 128
R = 256
LEV = 4
NZ, NC, NX, NY = 4, 2, 4, 4
BOTH = ("prow", "pcol")
WHOLE, HALF, SHORT = 32, 16, 8
ORDER = (2, 1, 3)


def pair_index(high, low):
    return high * (high - 1) // 2 + low


def device(z, c, x, y):
    return (z % NZ * NC + c) * NX * NY + x % NX * NY + y % NY


def shift_plane(value, step, phase):
    pairs = []
    for z in range(NZ):
        for c in range(NC):
            for x in range(NX):
                for y in range(NY):
                    if c == phase:
                        there = device(z, c, x + step, y)
                    else:
                        there = device(z, c, x, y + step)
                    pairs.append((device(z, c, x, y), there))
    return lax.ppermute(value, BOTH, pairs)


def shift_z(value, step):
    pairs = [(z * NC + c, (z + step) % NZ * NC + c) for z in range(NZ) for c in range(NC)]
    return lax.ppermute(value, "prow", pairs)


def swap_core(value):
    pairs = [(z * NC + c, z * NC + 1 - c) for z in range(NZ) for c in range(NC)]
    return lax.ppermute(value, "prow", pairs)


def split(value):
    high = value.astype(jnp.bfloat16)
    low = (value - high.astype(jnp.float32)).astype(jnp.bfloat16)
    return high, low


def near(value):
    return pltpu.with_memory_space_constraint(value, pltpu.VMEM)


def far(value):
    return pltpu.with_memory_space_constraint(value, pltpu.HBM)


def fast_call(kernel, shapes, operands, scalars, scratch, flops):
    return pl.pallas_call(
        kernel,
        in_specs=[pl.BlockSpec(memory_space=pltpu.SMEM)] * len(scalars)
        + [pl.BlockSpec(memory_space=pltpu.VMEM)] * len(operands),
        out_specs=[pl.BlockSpec(memory_space=pltpu.VMEM)] * len(shapes),
        out_shape=[pltpu.VMEM(shape, jnp.float32) for shape in shapes],
        scratch_shapes=scratch,
        compiler_params=pltpu.CompilerParams(vmem_limit_bytes=16 * 1024 * 1024),
        cost_estimate=pl.CostEstimate(flops=flops, bytes_accessed=4096, transcendentals=0),
    )(*scalars, *[near(value) for value in operands])


def pair_kernel(index, unroll, n_in, n_out, flip, has_init, waits, take, put, *refs):
    vectors, refs = refs[:n_in], refs[n_in:]
    blocks, refs = refs[0], refs[1:]
    init, refs = (refs[:n_out], refs[n_out:]) if has_init else ((), refs)
    refs = refs[waits:]
    outs, halves, total = refs[:n_out], refs[n_out], refs[n_out + 1]
    per = vectors[0].shape[0]
    for k in range(n_in):

        @pl.loop(0, per)
        def _(unit, k=k):
            high, low = split(vectors[k][unit])
            halves[k * per + unit, :W] = high
            halves[k * per + unit, W:] = low

    per = outs[0].shape[0]
    for k in range(n_out):

        @pl.loop(0, per)
        def _(unit, k=k):
            if has_init:
                total[k * per + unit] = init[k][unit]
            else:
                total[k * per + unit] = jnp.zeros((W, R), jnp.float32)

    @pl.loop(0, blocks.shape[1], step=unroll)
    def _(start):
        for j in range(unroll):
            slot = start + j
            block = blocks[index, slot]
            if flip:
                block = block.T
            high, low = split(block)
            left = jnp.concatenate(
                [jnp.concatenate([high, high], axis=1), jnp.concatenate([low, low], axis=1)], axis=0
            )
            product = jnp.dot(left, halves[take[slot]], preferred_element_type=jnp.float32)
            total[put[slot]] += product[:W] + product[W:]

    for k in range(n_out):

        @pl.loop(0, per)
        def _(unit, k=k):
            outs[k][unit] = total[k * per + unit]


def pair_product(index, unroll, flip, scalars, vectors, blocks, init, after, n_out, total):
    n_in = len(vectors)
    units = n_in * vectors[0].shape[0]
    return fast_call(
        functools.partial(pair_kernel, index, unroll, n_in, n_out, flip, init is not None, len(after)),
        [(total // n_out, W, R)] * n_out,
        [*vectors, blocks, *(init or ()), *after],
        scalars,
        [pltpu.VMEM((units, 2 * W, R), jnp.bfloat16), pltpu.VMEM((total, W, R), jnp.float32)],
        blocks.shape[1] * 8 * W * W * R,
    )


def dot(left, right):
    return jnp.dot(
        left, right, precision=lax.Precision.HIGHEST, preferred_element_type=jnp.float32
    )


def solve_kernel(level, flip, stacked, terms, inverse, base, *refs):
    value = base[level] if stacked else base[...]
    if terms:
        gone = refs[0][...]
        for ref in refs[1:terms]:
            gone = gone + ref[...]
        value = value - gone
    outs = refs[terms:]
    for flipped, out in zip(flip, outs):
        matrix = inverse[level]
        value = dot(matrix.T if flipped else matrix, value)
        out[...] = value


def solve(level, flip, inverse, base, gone):
    return fast_call(
        functools.partial(solve_kernel, level, flip, base.ndim == 3, len(gone)),
        [(W, R)] * len(flip),
        [inverse, base, *gone],
        [],
        [],
        12 * W * W * R,
    )


def add_kernel(terms, waits, *refs):
    for k, out in enumerate(refs[terms + waits :]):
        value = refs[0][k]
        for ref in refs[1:terms]:
            value = value + ref[k]
        out[...] = value


def add_units(parts, after):
    return fast_call(
        functools.partial(add_kernel, len(parts), len(after)),
        [(W, R)] * 4,
        [*parts, *after],
        [],
        [],
        len(parts) * 4 * W * R,
    )


def first_kernel(inverse, base, out, matrix, value, sems):
    copies = [
        pltpu.make_async_copy(inverse.at[0], matrix, sems.at[0]),
        pltpu.make_async_copy(base.at[0], value, sems.at[1]),
    ]
    for copy in copies:
        copy.start()
    for copy in copies:
        copy.wait()
    out[...] = dot(matrix[...], value[...])


def first_solve(inverse, base):
    return pl.pallas_call(
        first_kernel,
        in_specs=[pl.BlockSpec(memory_space=pl.ANY)] * 2,
        out_specs=pl.BlockSpec(memory_space=pltpu.VMEM),
        out_shape=pltpu.VMEM((W, R), jnp.float32),
        scratch_shapes=[
            pltpu.VMEM((W, W), jnp.float32),
            pltpu.VMEM((W, R), jnp.float32),
            pltpu.SemaphoreType.DMA((2,)),
        ],
        compiler_params=pltpu.CompilerParams(vmem_limit_bytes=16 * 1024 * 1024),
    )(far(inverse), far(base))


def load_kernel(live, blocks, after, out, sems):
    copies = [
        pltpu.make_async_copy(blocks.at[k], out.at[k], sems.at[k]) for k in range(blocks.shape[0])
    ]
    for copy in copies:
        copy.start()
    for k, copy in enumerate(copies):
        copy.wait()

        @pl.loop(0, blocks.shape[1])
        def _(slot, k=k):
            out[k, slot] = jnp.where(live[k, slot] > 0, out[k, slot], 0.0)


def load(live, blocks, after):
    return pl.pallas_call(
        load_kernel,
        in_specs=[
            pl.BlockSpec(memory_space=pltpu.SMEM),
            pl.BlockSpec(memory_space=pl.ANY),
            pl.BlockSpec(memory_space=pltpu.VMEM),
        ],
        out_specs=pl.BlockSpec(memory_space=pltpu.VMEM),
        out_shape=pltpu.VMEM(blocks.shape, jnp.float32),
        scratch_shapes=[pltpu.SemaphoreType.DMA((blocks.shape[0],))],
        compiler_params=pltpu.CompilerParams(vmem_limit_bytes=16 * 1024 * 1024),
        cost_estimate=pl.CostEstimate(
            flops=0, bytes_accessed=blocks.size * 4, transcendentals=0
        ),
    )(live, far(blocks), near(after))


def gather_plane(value):
    units = jnp.stack([value] + [shift_plane(value, d, 0) for d in ORDER])
    return [units] + [shift_plane(units, d, 1) for d in ORDER]


def scatter_plane(groups, beside):
    first = [shift_plane(groups[k], d, 0) for k, d in enumerate(ORDER, 1)]
    units = add_units([groups[0]] + first, beside(first[0]))
    return [units[0]] + [shift_plane(units[k], d, 1) for k, d in enumerate(ORDER, 1)]


def scatter_z(mine, other):
    units = add_units([mine, swap_core(other)], [])
    return [units[0]] + [shift_z(units[k], d) for k, d in enumerate(ORDER, 1)]


def gather_z(value):
    units = jnp.stack([value] + [shift_z(value, d) for d in ORDER])
    return [units, swap_core(units)]


def place(offset):
    spot = jnp.zeros_like(offset)
    for k, d in enumerate(ORDER, 1):
        spot = jnp.where(offset == d, k, spot)
    return spot


def body(rhs, dinv, blocks, targets, sources):
    right = rhs[:, 0, 0]
    inverse = dinv[:, 0, 0]
    aims = targets[0, 0]
    anchor = sources[0, 0]
    row = lax.axis_index("prow")
    col = lax.axis_index("pcol")
    z, core = row // NC, row % NC
    x, y = col // NY, col % NY
    live = (aims >= 0).astype(jnp.int32)
    rows = jnp.maximum(aims, 0)
    off_x = (x - anchor // NY) % NX
    off_y = (y - anchor % NY) % NY
    off_z = (z - rows // NC) % NZ
    first = core == 0
    from_x, from_y, from_z = [place(v) for v in (off_x, off_y, off_z)]
    to_x, to_y, to_z = [place((-v) % 4) for v in (off_x, off_y, off_z)]
    take_plane = jnp.where(first, from_y * NX + from_x, from_x * NY + from_y)
    put_plane = jnp.where(first, to_x * NY + to_y, to_y * NX + to_x)
    across = (rows % NC != core).astype(jnp.int32) * NZ
    take_z = across + from_z
    put_z = across + to_z

    def forth(high, low, vectors, init):
        index = pair_index(high, low)
        scalars = (take_plane[index], put_z[index])
        unroll = WHOLE if high == low + 1 else SHORT
        return pair_product(index, unroll, False, scalars, vectors, panels, init, (), 2, 8)

    def back(high, low, vectors, init, after):
        index = pair_index(high, low)
        scalars = (take_z[index], put_plane[index])
        unroll = WHOLE if high == low + 1 else HALF if high == LEV - 1 else SHORT
        return pair_product(index, unroll, True, scalars, vectors, panels, init, after, 4, 16)

    top = LEV - 1
    solved = [None] * LEV
    result = [None] * LEV
    sums = [None] * LEV
    for level in range(LEV):
        gone = [] if level == 0 else scatter_z(*sums[level])
        if level == top:
            solved[level], result[level] = solve(level, (False, True), inverse, right, gone)
            break
        if level == 0:
            solved[level] = first_solve(inverse, right)
        else:
            (solved[level],) = solve(level, (False,), inverse, right, gone)
        vectors = gather_plane(solved[level])
        if level == 0:
            panels = load(live, blocks[0, 0], vectors[0])
        for high in range(level + 1, LEV):
            sums[high] = forth(high, level, vectors, sums[high])
    sums = [None] * LEV
    for level in reversed(range(1, LEV)):
        vectors = gather_z(result[level])

        def beside(held):
            done = []
            for low in reversed(range(level - 1)):
                sums[low] = back(level, low, vectors, sums[low], (held,))
                done += sums[low][:1]
            return done

        gone = scatter_plane(back(level, level - 1, vectors, sums[level - 1], ()), beside)
        (result[level - 1],) = solve(level - 1, (True,), inverse, solved[level - 1], gone)
    forward = jnp.stack(solved)[:, None, None]
    solution = jnp.stack(result)[:, None, None]
    return (forward, solution)


def solution(mesh):
    placed = (
        P(None, "prow", "pcol", None, None),
        P(None, "prow", "pcol", None, None),
        P("prow", "pcol", None, None, None, None),
        P("prow", "pcol", None, None),
        P("prow", "pcol", None, None),
    )
    return jax.shard_map(
        body,
        mesh=mesh,
        in_specs=placed,
        out_specs=(P(None, "prow", "pcol", None, None), P(None, "prow", "pcol", None, None)),
        check_vma=False,
    )
```
